256 devices in a mesh: row: 16 (over y_lo, x, core), col: 16 (over z, y_hi).
Axes of the slice: x: 4, y: 4 (y_hi: 2, y_lo: 2; y = y_hi * 2 + y_lo), z: 8, core: 2. Of those that a mesh axis runs over, the one named last changes fastest.
Arguments:
- query_proj: bfloat16 [32, 1024, 768], P('row', 'col'), may hold values from -16 to 16
- key_proj: bfloat16 [32, 1024, 768], P('row', 'col'), may hold values from -16 to 16
- value_proj: bfloat16 [32, 1024, 768], P('row', 'col'), may hold values from -24 to 24
- grad_output: bfloat16 [32, 1024, 768], P('row', 'col'), may hold values from -48 to 48
Outputs:
- attended: bfloat16 [32, 1024, 768], P('row', 'col')
- grad_query: bfloat16 [32, 1024, 768], P('row', 'col')
- grad_key: bfloat16 [32, 1024, 768], P('row', 'col')
- grad_value: bfloat16 [32, 1024, 768], P('row', 'col')
The draws below stay inside these ranges and needn't reach their ends.
All inputs are finite; a program needn't handle non-finite values.
Results may differ from the reference program's by a relative error of at most 0.005.
Values may be sent and summed in bfloat16 or wider, within the bound.
A program may use at most 128 MiB of HBM per device.

```python
import math
import jax
import jax.numpy as jnp
from jax import lax

D = 768
H = 12
R = 32
C = 1024


def column_scales(key, lowest, highest):
    return jnp.exp(jax.random.uniform(key, (1, C, H, 1), jnp.float32, math.log(lowest), math.log(highest)))


def draw_query_proj(key, part):
    own_key = jax.random.fold_in(key, 11)
    scales = column_scales(jax.random.fold_in(own_key, 2), 0.5, 2.0)
    noise = jnp.clip(jax.random.normal(jax.random.fold_in(own_key, 1), (R, C, H, D // H), jnp.float32), -4.0, 4.0)
    return (noise * scales).reshape(R, C, D).astype(jnp.bfloat16)


def draw_key_proj(key, part):
    own_key = jax.random.fold_in(key, 23)
    scales = column_scales(jax.random.fold_in(own_key, 2), 0.3, 3.0)
    noise = jnp.clip(jax.random.normal(jax.random.fold_in(own_key, 1), (R, C, H, D // H), jnp.float32), -4.0, 4.0)
    return (noise * scales).reshape(R, C, D).astype(jnp.bfloat16)


def shard_levels(stream_key, extent, cuts, smallest, largest):
    loudness, own = 1.0, jax.random.fold_in(stream_key, 6)
    for dim, blocks in cuts:
        steps = jnp.exp(jax.random.uniform(jax.random.fold_in(own, dim), (blocks,), jnp.float32, smallest / len(cuts), largest / len(cuts)))
        loudness = loudness * jnp.repeat(steps, extent[dim] // blocks).reshape([-1 if axis == dim else 1 for axis in range(len(extent))])
    return loudness


def centred(key, shape, width, bound, pieces=(), held_as=jnp.bfloat16):
    drawn = jax.random.normal(key, shape, jnp.float32) * width
    if len(pieces) > 0:
        drawn = shard_levels(key, shape, pieces, -0.22, 0.18) * drawn
    return jnp.clip(drawn, min=-bound, max=bound).astype(held_as)


def setup_inputs(seed: int = 0) -> dict:
    splits = jax.random.split(jax.random.key(seed), 5)
    return {
        "query_proj": draw_query_proj(jax.random.fold_in(splits[4], 71), 0),
        "key_proj": draw_key_proj(jax.random.fold_in(splits[4], 71), 0),
        "value_proj": centred(splits[2], (R, C, D), 4.0, 24.0, ((0, 16), (1, 16))),
        "grad_output": centred(splits[3], (R, C, D), 8.0, 48.0, ((0, 16), (1, 16))),
    }


def split_heads(array):
    return array.astype(jnp.float32).reshape(array.shape[0], array.shape[1], H, D // H)

def reference(query_proj, key_proj, value_proj, grad_output):
    factor = 1.0 / math.sqrt(D // H * R)
    query_heads = split_heads(query_proj)
    key_heads = split_heads(key_proj)
    value_heads = split_heads(value_proj)
    grad_heads = split_heads(grad_output)
    logits = jnp.einsum('rihe,rjhe->hij', query_heads, key_heads) * factor
    attn_weights = jax.nn.softmax(logits, axis=-1)
    weights_b = attn_weights.astype(jnp.bfloat16)
    weights_wide = weights_b.astype(jnp.float32)
    attended = jnp.einsum('hij,rjhe->rihe', weights_wide, value_heads).astype(jnp.bfloat16).reshape(R, C, D)
    dprobs = jnp.einsum('rihe,rjhe->hij', grad_heads, value_heads)
    row_dot = lax.optimization_barrier(jnp.sum(attn_weights * dprobs, axis=-1, keepdims=True))
    dscores = (factor * attn_weights * (dprobs - row_dot)).astype(jnp.bfloat16)
    dscore_wide = dscores.astype(jnp.float32)
    grad_query = jnp.einsum('hij,rjhe->rihe', dscore_wide, key_heads).astype(jnp.bfloat16).reshape(R, C, D)
    key_total = jnp.einsum('hij,rihe->rjhe', dscore_wide, query_heads)
    value_total = jnp.einsum('hij,rihe->rjhe', weights_wide, grad_heads)
    grad_key = key_total.astype(jnp.bfloat16).reshape(R, C, D)
    grad_value = value_total.astype(jnp.bfloat16).reshape(R, C, D)
    return (attended, grad_query, grad_key, grad_value)
```

```python
import functools
import math

import jax
import jax.numpy as jnp
from jax import lax
from jax.experimental import pallas as pl
from jax.experimental.pallas import tpu as pltpu
from jax.sharding import PartitionSpec as P

D = 768
H = 12
HG = 3
NX = 4
NZ = 8
C = 64
W = 512
MESH = pl.DeviceIdType.MESH
BF = jnp.bfloat16
F32 = jnp.float32


def swap_halves(first, second):
    half = first.shape[-1] // 2
    low = jnp.concatenate([first[:, :half], second[:, :half]], axis=1)
    high = jnp.concatenate([first[:, half:], second[:, half:]], axis=1)
    return low, high


def kernel(
    factor,
    q_ref, k_ref, v_ref, g_ref,
    a_out, gq_out, gk_out, gv_out,
    rep, kv, qg, part, part_in, stat, stat_in, probs, mine, eacc, edge, edge_in,
    rterm, rsend, rrecv, fin, orep,
    send_sems, recv_sems,
):
    row, col = lax.axis_index("row"), lax.axis_index("col")
    ylo, x, core = row // 8, (row // 2) % NX, row % 2
    z, yhi = col // 2, col % 2
    quarter = ylo * 2 + core

    def device(x_=None, ylo_=None, core_=None, z_=None, yhi_=None):
        x_ = x if x_ is None else x_
        ylo_ = ylo if ylo_ is None else ylo_
        core_ = core if core_ is None else core_
        z_ = z if z_ is None else z_
        yhi_ = yhi if yhi_ is None else yhi_
        return (ylo_ * 8 + x_ * 2 + core_, z_ * 2 + yhi_)

    xs = [lax.rem(x + k, NX) for k in range(NX)]
    x_peers = [device(x_=xs[k]) for k in (1, 2, 3)]
    right, left = device(z_=lax.rem(z + 1, NZ)), device(z_=lax.rem(z + NZ - 1, NZ))
    partner = device(yhi_=1 - yhi)
    group = []
    for k in (1, 2, 3):
        ylo_k, core_k = lax.rem(ylo + k // 2, 2), lax.rem(core + k % 2, 2)
        group.append((device(ylo_=ylo_k, core_=core_k), ylo_k * 2 + core_k))

    barrier = pltpu.get_barrier_semaphore()
    peers = x_peers + [right, left, partner] + [peer for peer, _ in group]
    for peer in peers:
        pl.semaphore_signal(barrier, inc=1, device_id=peer, device_id_type=MESH)

    count = [0]
    started = []

    def remote(src, dst, peer):
        index = count[0]
        count[0] += 1
        copy = pltpu.make_async_remote_copy(
            src_ref=src, dst_ref=dst, send_sem=send_sems.at[index], recv_sem=recv_sems.at[index],
            device_id=peer, device_id_type=MESH,
        )
        copy.start()
        started.append(copy)
        return copy

    def zblock(offset):
        return pl.multiple_of(lax.rem(z + offset + NZ, NZ) * C, C)

    def lanes(x_):
        return pl.ds(pl.multiple_of(x_ * 128, 128), 128)

    for array, ref in enumerate((k_ref, v_ref, q_ref, g_ref)):
        for m in range(H // 2):
            tile = slice(128 * m, 128 * m + 128)
            low, high = swap_halves(ref[0, :, tile], ref[1, :, tile])
            rep[array, 2 * m] = low
            rep[array, 2 * m + 1] = high

    pl.semaphore_wait(barrier, len(peers))

    own = pl.ds(zblock(0), C)
    ours = pl.ds(pl.multiple_of(yhi * C, C), C)
    theirs = pl.ds(pl.multiple_of((1 - yhi) * C, C), C)
    rows_q = pl.ds(pl.multiple_of(quarter * 32, 32), 32)

    kv_in, qg_in = {}, {}

    def x_in(h):
        kv_in[h] = [
            remote(rep.at[pl.ds(0, 2), xs[k] * HG + h], kv.at[:, h, own, lanes(x)], x_peers[k - 1])
            for k in (1, 2, 3)
        ]
        qg_in[h] = [
            remote(rep.at[pl.ds(2, 2), xs[k] * HG + h], qg.at[:, h, ours, lanes(x)], x_peers[k - 1])
            for k in (1, 2, 3)
        ]
        for t in range(2):
            kv[t, h, own, lanes(x)] = rep[t, x * HG + h]
            qg[t, h, ours, lanes(x)] = rep[2 + t, x * HG + h]

    ring = {}

    def ag_send(h, t, step):
        full = step < 4
        right_block = zblock(1 - step)
        left_block = zblock(step - 1)
        size = C if full else C // 2
        there = kv.at[t, h, pl.ds(right_block, size)]
        back = kv.at[t, h, pl.ds(left_block if full else left_block + C // 2, size)]
        ring[h, t, step] = (remote(there, there, right), remote(back, back, left))

    def ag_start(h):
        for copy in kv_in[h]:
            copy.wait_recv()
        for t in range(2):
            ag_send(h, t, 1)

    def ag_step(h, step):
        for t in range(2):
            for copy in ring[h, t, step]:
                copy.wait_recv()
            if step < 4:
                ag_send(h, t, step + 1)

    qg_swap = {}

    def qg_start(h):
        for copy in qg_in[h]:
            copy.wait_recv()
        half = qg.at[:, h, ours]
        qg_swap[h] = remote(half, half, partner)

    part_copies = {}

    def s_compute(h):
        qg_swap[h].wait_recv()
        for t in range(2):
            part[t, h] = lax.dot_general(
                qg[t, h], kv[t, h], (((1,), (1,)), ((), ())), preferred_element_type=F32
            )
        part_copies[h] = [
            remote(
                part.at[:, h, pl.ds(pl.multiple_of(theirs_q * 32, 32), 32)], part_in.at[:, h, k], peer
            )
            for k, (peer, theirs_q) in enumerate(group)
        ]

    stat_copies = {}

    def s_reduce(h):
        for copy in part_copies[h]:
            copy.wait_recv()
        score, dprob = (
            (part[t, h, rows_q] + part_in[t, h, 0]) + (part_in[t, h, 1] + part_in[t, h, 2])
            for t in range(2)
        )
        score = score * factor
        top = jnp.max(score, axis=1, keepdims=True)
        weight = jnp.exp(score - top)
        total = jnp.sum(weight, axis=1, keepdims=True)
        dot = jnp.sum(weight * dprob, axis=1, keepdims=True)
        mine[0, h] = weight
        mine[1, h] = dprob
        lane = lax.broadcasted_iota(jnp.int32, (32, 128), 1)
        stat[h] = jnp.where(lane == 0, top, jnp.where(lane == 1, total, dot))
        stat_copies[h] = remote(stat.at[h], stat_in.at[h], partner)

    probs_copies = {}

    def p_compute(h):
        stat_copies[h].wait_recv()
        here, there = stat[h], stat_in[h]
        top_a, total_a, dot_a = here[:, 0:1], here[:, 1:2], here[:, 2:3]
        top_b, total_b, dot_b = there[:, 0:1], there[:, 1:2], there[:, 2:3]
        top = jnp.maximum(top_a, top_b)
        scale_a, scale_b = jnp.exp(top_a - top), jnp.exp(top_b - top)
        total = total_a * scale_a + total_b * scale_b
        row_dot = (dot_a * scale_a + dot_b * scale_b) / total
        weights = mine[0, h] * (scale_a / total)
        probs[0, h, rows_q] = weights.astype(BF)
        probs[1, h, rows_q] = (factor * weights * (mine[1, h] - row_dot)).astype(BF)
        block = probs.at[:, h, rows_q]
        probs_copies[h] = [remote(block, block, peer) for peer, _ in group]

    edge_copies = {}
    sums = {}

    def rs_send(h, t, step):
        for way, peer in ((0, right), (1, left)):
            offset = (5 - step) * (1 if way == 0 else -1)
            start = zblock(offset)
            if step == 1:
                half = C // 2 * way
                rsend[t, h, way, 0, half : half + C // 2] = rterm[
                    t, h, pl.ds(start + half, C // 2)
                ].astype(BF)
                src, dst = (
                    ref.at[t, h, way, 0, pl.ds(half, C // 2)] for ref in (rsend, rrecv)
                )
            else:
                sums[h, t, step - 1][way].wait_recv()
                term = rterm[t, h, pl.ds(start, C)]
                if step == 2:
                    half = C // 2 * way
                    other = C // 2 - half
                    rsend[t, h, way, 1, half : half + C // 2] = (
                        rterm[t, h, pl.ds(start + half, C // 2)]
                        + rrecv[t, h, way, 0, half : half + C // 2].astype(F32)
                    ).astype(BF)
                    rsend[t, h, way, 1, other : other + C // 2] = rterm[
                        t, h, pl.ds(start + other, C // 2)
                    ].astype(BF)
                else:
                    rsend[t, h, way, step - 1] = (
                        term + rrecv[t, h, way, step - 2].astype(F32)
                    ).astype(BF)
                src, dst = rsend.at[t, h, way, step - 1], rrecv.at[t, h, way, step - 1]
            sums.setdefault((h, t, step), []).append(remote(src, dst, peer))

    def out_compute(h):
        for copy in probs_copies[h]:
            copy.wait_recv()
        for t, (p, other) in enumerate(((1, 0), (0, 1))):
            rterm[t, h] = lax.dot_general(
                probs[p, h], qg[other, h], (((0,), (0,)), ((), ())), preferred_element_type=F32
            )
            rs_send(h, t, 1)
        for t, (p, other) in enumerate(((0, 1), (1, 0))):
            eacc[t, h] = jnp.dot(probs[p, h], kv[other, h], preferred_element_type=F32)
            edge[t, h] = eacc[t, h, theirs].astype(BF)
        edge_copies[h] = remote(edge.at[:, h], edge_in.at[:, h], partner)

    out_copies = []

    def x_out(h, first):
        out_copies.extend(
            remote(
                fin.at[pl.ds(first, 2), h, :, lanes(xs[k])],
                orep.at[pl.ds(first, 2), x * HG + h],
                x_peers[k - 1],
            )
            for k in (1, 2, 3)
        )
        for t in range(2):
            orep[first + t, x * HG + h] = fin[first + t, h, :, lanes(x)]

    def edge_end(h):
        edge_copies[h].wait_recv()
        for t in range(2):
            fin[t, h] = (eacc[t, h, ours] + edge_in[t, h].astype(F32)).astype(BF)
        x_out(h, 0)

    def rs_step(h, step):
        for t in range(2):
            rs_send(h, t, step)

    def rs_end(h):
        for t in range(2):
            for copy in sums[h, t, 4]:
                copy.wait_recv()
            fin[2 + t, h] = (
                rterm[t, h, own]
                + (rrecv[t, h, 0, 3].astype(F32) + rrecv[t, h, 1, 3].astype(F32))
            ).astype(BF)
        x_out(h, 2)

    for h in range(HG):
        x_in(h)
    ag_start(0)
    qg_start(0)
    ag_step(0, 1)
    ag_step(0, 2)
    ag_start(1)
    qg_start(1)
    ag_step(0, 3)
    ag_step(1, 1)
    ag_step(0, 4)
    s_compute(0)
    ag_step(1, 2)
    ag_start(2)
    qg_start(2)
    s_reduce(0)
    ag_step(1, 3)
    p_compute(0)
    ag_step(2, 1)
    ag_step(1, 4)
    s_compute(1)
    ag_step(2, 2)
    out_compute(0)
    s_reduce(1)
    ag_step(2, 3)
    p_compute(1)
    rs_step(0, 2)
    edge_end(0)
    ag_step(2, 4)
    s_compute(2)
    out_compute(1)
    rs_step(0, 3)
    s_reduce(2)
    rs_step(1, 2)
    rs_step(0, 4)
    p_compute(2)
    edge_end(1)
    rs_step(1, 3)
    out_compute(2)
    rs_end(0)
    rs_step(1, 4)
    rs_step(2, 2)
    edge_end(2)
    rs_end(1)
    rs_step(2, 3)
    rs_step(2, 4)
    rs_end(2)

    for copy in out_copies:
        copy.wait_recv()
    for array, ref in enumerate((a_out, gq_out, gk_out, gv_out)):
        for m in range(H // 2):
            tile = slice(128 * m, 128 * m + 128)
            first, second = swap_halves(orep[array, 2 * m], orep[array, 2 * m + 1])
            ref[0, :, tile] = first
            ref[1, :, tile] = second
    for copy in started:
        copy.wait_send()


COPIES = 18 + 48 + 3 + 9 + 3 + 9 + 3 + 48 + 18


def shards(query_proj, key_proj, value_proj, grad_output):
    row_count = query_proj.shape[0] * lax.axis_size("row")
    factor = 1.0 / math.sqrt(D // H * row_count)
    vmem = pl.BlockSpec(memory_space=pltpu.VMEM)
    shape = jax.ShapeDtypeStruct(query_proj.shape, BF)
    return pl.pallas_call(
        functools.partial(kernel, factor),
        out_shape=(shape,) * 4,
        in_specs=[vmem] * 4,
        out_specs=(vmem,) * 4,
        scratch_shapes=[
            pltpu.VMEM((4, H, C, 128), BF),
            pltpu.VMEM((2, HG, NZ * C, W), BF),
            pltpu.VMEM((2, HG, 2 * C, W), BF),
            pltpu.VMEM((2, HG, 2 * C, W), F32),
            pltpu.VMEM((2, HG, 3, 32, W), F32),
            pltpu.VMEM((HG, 32, 128), F32),
            pltpu.VMEM((HG, 32, 128), F32),
            pltpu.VMEM((2, HG, 2 * C, W), BF),
            pltpu.VMEM((2, HG, 32, W), F32),
            pltpu.VMEM((2, HG, 2 * C, W), F32),
            pltpu.VMEM((2, HG, C, W), BF),
            pltpu.VMEM((2, HG, C, W), BF),
            pltpu.VMEM((2, HG, NZ * C, W), F32),
            pltpu.VMEM((2, HG, 2, 4, C, W), BF),
            pltpu.VMEM((2, HG, 2, 4, C, W), BF),
            pltpu.VMEM((4, HG, C, W), BF),
            pltpu.VMEM((4, H, C, 128), BF),
            pltpu.SemaphoreType.DMA((COPIES,)),
            pltpu.SemaphoreType.DMA((COPIES,)),
        ],
        compiler_params=pltpu.CompilerParams(
            collective_id=0, has_side_effects=True, vmem_limit_bytes=56 * 2**20
        ),
        cost_estimate=pl.CostEstimate(flops=1_208_000_000, bytes_accessed=1_600_000, transcendentals=50_000),
    )(query_proj, key_proj, value_proj, grad_output)


def solution(mesh):
    placed = P("row", "col", None)
    return jax.shard_map(
        shards,
        mesh=mesh,
        in_specs=(placed,) * 4,
        out_specs=(placed,) * 4,
        check_vma=False,
    )
```

```python
import functools
import math

import jax
import jax.numpy as jnp
from jax import lax
from jax.experimental import pallas as pl
from jax.experimental.pallas import tpu as pltpu
from jax.sharding import PartitionSpec as P

D = 768
H = 12
NX = 4
NZ = 8
C = 64
W = 512
J = 512
MESH = pl.DeviceIdType.MESH
BF = jnp.bfloat16
F32 = jnp.float32

ATTENDED, GRAD_QUERY, GRAD_KEY, GRAD_VALUE = range(4)


def swap_halves(first, second):
    half = first.shape[-1] // 2
    low = jnp.concatenate([first[:, :half], second[:, :half]], axis=1)
    high = jnp.concatenate([first[:, half:], second[:, half:]], axis=1)
    return low, high


def nt_dot(a, b):
    return lax.dot_general(a, b, (((1,), (1,)), ((), ())), preferred_element_type=F32)


def tn_dot(a, b):
    return lax.dot_general(a, b, (((0,), (0,)), ((), ())), preferred_element_type=F32)


class Unit:
    def __init__(self, net, n, cb, me, right, left, refs):
        self.net, self.n, self.cb, self.me = net, n, cb, me
        self.right, self.left = right, left
        (
            self.kv, self.qg, self.part, self.core_in, self.half, self.ylo_in, self.stat, self.stat_in,
            self.probs, self.mine, self.eacc, self.edge, self.edge_in, self.rterm, self.rsend,
            self.rrecv, self.fin,
        ) = refs
        self.ours = pl.ds(pl.multiple_of(net.yhi * cb, cb), cb)
        self.theirs = pl.ds(pl.multiple_of((1 - net.yhi) * cb, cb), cb)
        self.own = pl.ds(self.block(0), cb)
        self.quarter = cb // 2
        self.rows_q = pl.ds(
            pl.multiple_of(net.core * cb + net.ylo * self.quarter, self.quarter), self.quarter
        )
        self.ring, self.swap, self.core_copy, self.ylo_copy = {}, {}, {}, {}
        self.stat_copy, self.probs_copy, self.edge_copy, self.sums = {}, {}, {}, {}

    @staticmethod
    def scratch(n, cb):
        return [
            pltpu.VMEM((2, J, W), BF),
            pltpu.VMEM((2, 2 * cb, W), BF),
            pltpu.VMEM((2, 2 * cb, J), F32),
            pltpu.VMEM((2, cb, J), F32),
            pltpu.VMEM((2, cb, J), F32),
            pltpu.VMEM((2, cb // 2, J), F32),
            pltpu.VMEM((2, cb // 2, 128), F32),
            pltpu.VMEM((2, cb // 2, 128), F32),
            pltpu.VMEM((2, 2 * cb, J), BF),
            pltpu.VMEM((2, cb // 2, J), F32),
            pltpu.VMEM((2, 2 * cb, W), F32),
            pltpu.VMEM((2, cb, W), BF),
            pltpu.VMEM((2, cb, W), BF),
            pltpu.VMEM((2, J, W), F32),
            pltpu.VMEM((2, 2, n // 2, cb, W), BF),
            pltpu.VMEM((2, 2, n // 2, cb, W), BF),
            pltpu.VMEM((4, cb, W), BF),
        ]

    def block(self, offset):
        return pl.multiple_of(lax.rem(self.me + offset + self.n, self.n) * self.cb, self.cb)

    def ring_send(self, t, step):
        full = step < self.n // 2
        size = self.cb if full else self.cb // 2
        left_block = self.block(step - 1)
        there = self.kv.at[t, pl.ds(self.block(1 - step), size)]
        back = self.kv.at[t, pl.ds(left_block if full else left_block + self.cb // 2, size)]
        self.ring[t, step] = (
            self.net.remote(there, there, self.right),
            self.net.remote(back, back, self.left),
        )

    def ring_step(self, t, step):
        for copy in self.ring[t, step]:
            copy.wait_recv()
        if step < self.n // 2:
            self.ring_send(t, step + 1)

    def swap_start(self, t):
        mine = self.qg.at[t, self.ours]
        self.swap[t] = self.net.remote(mine, mine, self.net.partner)

    def s_compute(self, t):
        self.swap[t].wait_recv()
        self.part[t] = nt_dot(self.qg[t], self.kv[t])
        other = pl.ds(pl.multiple_of((1 - self.net.core) * self.cb, self.cb), self.cb)
        self.core_copy[t] = self.net.remote(
            self.part.at[t, other], self.core_in.at[t], self.net.core_peer
        )

    def s_core(self, t):
        self.core_copy[t].wait_recv()
        rows = pl.ds(pl.multiple_of(self.net.core * self.cb, self.cb), self.cb)
        self.half[t] = self.part[t, rows] + self.core_in[t]
        other = pl.ds(
            pl.multiple_of((1 - self.net.ylo) * self.quarter, self.quarter), self.quarter
        )
        self.ylo_copy[t] = self.net.remote(
            self.half.at[t, other], self.ylo_in.at[t], self.net.ylo_peer
        )

    def s_reduce(self, t):
        self.ylo_copy[t].wait_recv()
        rows = pl.ds(pl.multiple_of(self.net.ylo * self.quarter, self.quarter), self.quarter)
        total = self.half[t, rows] + self.ylo_in[t]
        if t == 0:
            score = total * self.net.factor
            top = jnp.max(score, axis=1, keepdims=True)
            weight = jnp.exp(score - top)
            self.mine[0] = weight
            lane = lax.broadcasted_iota(jnp.int32, (self.quarter, 128), 1)
            self.stat[0] = jnp.where(lane == 0, top, jnp.sum(weight, axis=1, keepdims=True))
        else:
            self.mine[1] = total
            dot = jnp.sum(self.mine[0] * total, axis=1, keepdims=True)
            self.stat[1] = jnp.broadcast_to(dot, (self.quarter, 128))
        self.stat_copy[t] = self.net.remote(
            self.stat.at[t], self.stat_in.at[t], self.net.partner
        )

    def p_compute(self, t):
        self.stat_copy[t].wait_recv()
        here, there = self.stat[t], self.stat_in[t]
        if t == 0:
            top_a, top_b = here[:, 0:1], there[:, 0:1]
            top = jnp.maximum(top_a, top_b)
            scale_a, scale_b = jnp.exp(top_a - top), jnp.exp(top_b - top)
            total = here[:, 1:2] * scale_a + there[:, 1:2] * scale_b
            weights = self.mine[0] * (scale_a / total)
            self.mine[0] = weights
            self.probs[0, self.rows_q] = weights.astype(BF)
        else:
            row_dot = here[:, 0:1] + there[:, 0:1]
            self.probs[1, self.rows_q] = (
                self.net.factor * self.mine[0] * (self.mine[1] - row_dot)
            ).astype(BF)
        block = self.probs.at[t, self.rows_q]
        self.probs_copy[t] = [
            self.net.remote(block, block, peer)
            for peer in (self.net.ylo_peer, self.net.far_peer, self.net.core_peer)
        ]

    def out_compute(self, t):
        for copy in self.probs_copy[t]:
            copy.wait_recv()
        self.rterm[t] = tn_dot(self.probs[t], self.qg[1 - t])
        self.rs_send(t, 1)
        self.eacc[t] = jnp.dot(self.probs[t], self.kv[1 - t], preferred_element_type=F32)
        self.edge[t] = self.eacc[t, self.theirs].astype(BF)
        self.edge_copy[t] = self.net.remote(
            self.edge.at[t], self.edge_in.at[t], self.net.partner
        )

    def rs_send(self, t, step):
        cb, half = self.cb, self.cb // 2
        for way, peer in ((0, self.right), (1, self.left)):
            start = self.block((self.n // 2 + 1 - step) * (1 if way == 0 else -1))
            first, rest = slice(half * way, half * way + half), slice(half - half * way, cb - half * way)
            send = self.rsend.at[t, way, step - 1]
            recv = self.rrecv.at[t, way, step - 1]
            if step == 1:
                send[first] = self.rterm[t, pl.ds(start + half * way, half)].astype(BF)
                send, recv = (ref.at[pl.ds(half * way, half)] for ref in (send, recv))
            else:
                self.sums[t, step - 1][way].wait_recv()
                arrived = self.rrecv.at[t, way, step - 2]
                if step == 2:
                    send[first] = (
                        self.rterm[t, pl.ds(start + half * way, half)] + arrived[first].astype(F32)
                    ).astype(BF)
                    send[rest] = self.rterm[t, pl.ds(start + half - half * way, half)].astype(BF)
                else:
                    send[...] = (
                        self.rterm[t, pl.ds(start, cb)] + arrived[...].astype(F32)
                    ).astype(BF)
            self.sums.setdefault((t, step), []).append(self.net.remote(send, recv, peer))

    def rs_end(self, t):
        last = self.n // 2
        for copy in self.sums[t, last]:
            copy.wait_recv()
        index = (GRAD_VALUE, GRAD_KEY)[t]
        self.fin[index] = (
            self.rterm[t, self.own]
            + (self.rrecv[t, 0, last - 1].astype(F32) + self.rrecv[t, 1, last - 1].astype(F32))
        ).astype(BF)
        self.out_send(index)

    def edge_end(self, t):
        self.edge_copy[t].wait_recv()
        index = (ATTENDED, GRAD_QUERY)[t]
        self.fin[index] = (
            self.eacc[t, self.ours] + self.edge_in[t].astype(F32)
        ).astype(BF)
        self.out_send(index)


class XUnit(Unit):
    def in_send(self, t):
        net = self.net
        lanes = net.lanes(net.x)
        self.arrive = getattr(self, "arrive", {})
        for name, array, ref, rows in ((0, t, self.kv, self.own), (1, 2 + t, self.qg, self.ours)):
            self.arrive[name, t] = [
                net.remote(net.rep.at[array, NZ + net.xs[k]], ref.at[t, rows, lanes], net.x_peers[k])
                for k in (2, 1, 3)
            ]
            ref[t, rows, lanes] = net.rep[array, NZ + net.x]

    def in_wait(self, name, t):
        for copy in self.arrive[name, t]:
            copy.wait_recv()

    def out_send(self, index):
        net = self.net
        self.leave = getattr(self, "leave", {})
        self.leave[index] = [
            net.remote(
                self.fin.at[index, :, net.lanes(net.xs[k])], net.orep.at[index, NZ + net.x], net.x_peers[k]
            )
            for k in (2, 1, 3)
        ]
        net.orep[index, NZ + net.x] = self.fin[index, :, net.lanes(net.x)]

    def out_wait(self, index):
        for copy in self.leave[index]:
            copy.wait_recv()


class ZUnit(Unit):
    def in_send(self, t):
        net = self.net
        lanes = net.lanes(net.x)
        self.arrive = getattr(self, "arrive", {})
        slot = net.x * 2 + lax.rem(net.z, 2)
        sub = lax.rem(net.z, 2) * C
        bases = [net.take(NZ), net.take(NZ)]
        for k in (4, 3, 5, 2, 6, 1, 7, 0):
            z_to = lax.rem(net.z + k, NZ)
            x_to = lax.rem(net.z // 2 + z_to, NX)
            alone = None if k else x_to == net.x
            for name, array, ref, start in (
                (0, t, self.kv, x_to * self.cb),
                (1, 2 + t, self.qg, net.yhi * self.cb),
            ):
                dst = ref.at[t, pl.ds(pl.multiple_of(start + sub, C), C), lanes]
                net.remote(
                    net.rep.at[array, z_to], dst, net.device(x=x_to, z=z_to),
                    recv=bases[name] + slot, alone=alone,
                )
        for name, ref in ((0, self.kv), (1, self.qg)):
            self.arrive[name, t] = [
                (ref.at[t, pl.ds(0, C), pl.ds(0, 128)], bases[name] + k) for k in range(NZ)
            ]

    def in_wait(self, name, t):
        for ref, index in self.arrive[name, t]:
            self.net.wait_recv(ref, index)

    def out_send(self, index):
        net = self.net
        self.leave = getattr(self, "leave", {})
        pair = lax.rem(net.x - net.z + NZ, NX)
        base = net.take(NZ)
        for k in (2, 1, 3, 0):
            for s in range(2):
                z_to = pair * 2 + s
                net.remote(
                    self.fin.at[index, pl.ds(s * C, C), net.lanes(net.xs[k])],
                    net.orep.at[index, net.z],
                    net.device(x=net.xs[k], z=z_to),
                    recv=base + net.z, alone=None if k else z_to == net.z,
                )
        self.leave[index] = [(net.orep.at[index, k], base + k) for k in range(NZ)]

    def out_wait(self, index):
        for ref, slot in self.leave[index]:
            self.net.wait_recv(ref, slot)


class Net:
    def __init__(self, factor, rep, orep, send_sems, recv_sems):
        self.factor, self.rep, self.orep = factor, rep, orep
        self.send_sems, self.recv_sems = send_sems, recv_sems
        row, col = lax.axis_index("row"), lax.axis_index("col")
        self.ylo, self.x, self.core = row // 8, lax.rem(row // 2, NX), lax.rem(row, 2)
        self.z, self.yhi = col // 2, lax.rem(col, 2)
        self.xs = [lax.rem(self.x + k, NX) for k in range(NX)]
        self.x_peers = [self.device(x=x) for x in self.xs]
        self.partner = self.device(yhi=1 - self.yhi)
        self.core_peer = self.device(core=1 - self.core)
        self.ylo_peer = self.device(ylo=1 - self.ylo)
        self.far_peer = self.device(ylo=1 - self.ylo, core=1 - self.core)
        self.sent, self.received, self.started = 0, 0, []

    def device(self, **at):
        ylo, x, core, z, yhi = (at.get(k, getattr(self, k)) for k in ("ylo", "x", "core", "z", "yhi"))
        return (ylo * 8 + x * 2 + core, z * 2 + yhi)

    def lanes(self, x):
        return pl.ds(pl.multiple_of(x * 128, 128), 128)

    def take(self, n):
        self.received += n
        return self.received - n

    def remote(self, src, dst, peer, recv=None, alone=None):
        recv = self.take(1) if recv is None else recv
        send = self.send_sems.at[self.sent]
        self.sent += 1
        copy = pltpu.make_async_remote_copy(
            src_ref=src, dst_ref=dst, send_sem=send, recv_sem=self.recv_sems.at[recv],
            device_id=peer, device_id_type=MESH,
        )
        if alone is None:
            copy.start()
        else:
            pl.when(jnp.logical_not(alone))(copy.start)
            pl.when(alone)(pltpu.make_async_copy(src, dst, self.recv_sems.at[recv]).start)
        self.started.append((copy, alone))
        return copy

    def wait_recv(self, ref, index):
        pltpu.make_async_copy(ref, ref, self.recv_sems.at[index]).wait()

    def finish(self):
        for copy, alone in self.started:
            if alone is None:
                copy.wait_send()
            else:
                pl.when(jnp.logical_not(alone))(copy.wait_send)


def kernel(factor, q_ref, k_ref, v_ref, g_ref, orep, rep, send_sems, recv_sems, *refs):
    net = Net(factor, rep, orep, send_sems, recv_sems)
    count = len(refs) // 2
    small = XUnit(
        net, NZ, C, net.z,
        net.device(z=lax.rem(net.z + 1, NZ)), net.device(z=lax.rem(net.z + NZ - 1, NZ)), refs[:count],
    )
    big = ZUnit(net, NX, 2 * C, net.x, net.x_peers[1], net.x_peers[3], refs[count:])

    barrier = pltpu.get_barrier_semaphore()

    def greet(peer):
        pl.semaphore_signal(barrier, inc=1, device_id=peer, device_id_type=MESH)

    near = net.x_peers[1:] + [small.right, small.left, net.partner, net.core_peer, net.ylo_peer, net.far_peer]
    pair = lax.rem(net.x - net.z + NZ, NX)
    for k in (2, 1, 3, 0):
        for s in range(2):
            peer = net.device(x=net.xs[k], z=pair * 2 + s)
            if k:
                greet(peer)
            else:
                pl.when(pair * 2 + s != net.z)(functools.partial(greet, peer))
    for peer in near:
        greet(peer)

    for array, ref in ((0, k_ref), (2, q_ref), (1, v_ref), (3, g_ref)):
        for m in range(H // 2):
            tile = slice(128 * m, 128 * m + 128)
            low, high = swap_halves(ref[0, :, tile], ref[1, :, tile])
            rep[array, 2 * m] = low
            rep[array, 2 * m + 1] = high

    alone = (lax.rem(net.z // 2 + net.z, NX) == net.x).astype(jnp.int32)
    pl.semaphore_wait(barrier, len(near) + NZ - alone)

    for t in range(2):
        small.in_send(t)
        big.in_send(t)

    def ring_start(unit, t):
        unit.in_wait(0, t)
        unit.ring_send(t, 1)

    def swap_start(unit, t):
        unit.in_wait(1, t)
        unit.swap_start(t)

    ring_start(small, 0)
    swap_start(small, 0)
    ring_start(small, 1)
    swap_start(small, 1)
    ring_start(big, 0)
    swap_start(big, 0)
    small.ring_step(0, 1)
    small.ring_step(1, 1)
    small.ring_step(0, 2)
    ring_start(big, 1)
    swap_start(big, 1)
    big.ring_step(0, 1)
    small.ring_step(1, 2)
    small.ring_step(0, 3)
    big.ring_step(0, 2)
    big.s_compute(0)
    small.ring_step(1, 3)
    big.ring_step(1, 1)
    big.s_core(0)
    small.ring_step(0, 4)
    small.s_compute(0)
    small.ring_step(1, 4)
    small.s_core(0)
    big.ring_step(1, 2)
    big.s_compute(1)
    small.s_compute(1)
    big.s_core(1)
    small.s_core(1)
    big.s_reduce(0)
    small.s_reduce(0)
    big.p_compute(0)
    small.p_compute(0)
    big.s_reduce(1)
    small.s_reduce(1)
    big.out_compute(0)
    small.out_compute(0)
    big.p_compute(1)
    small.p_compute(1)
    big.rs_send(0, 2)
    small.rs_send(0, 2)
    big.out_compute(1)
    small.out_compute(1)
    small.rs_send(0, 3)
    big.edge_end(0)
    small.edge_end(0)
    big.rs_end(0)
    small.rs_send(1, 2)
    big.rs_send(1, 2)
    small.rs_send(0, 4)
    small.rs_send(1, 3)
    big.edge_end(1)
    small.edge_end(1)
    big.rs_end(1)
    small.rs_end(0)
    small.rs_send(1, 4)
    small.rs_end(1)

    for unit in (big, small):
        for index in range(4):
            unit.out_wait(index)
    net.finish()


def repack(orep, *outs):
    for array, ref in enumerate(outs):
        for m in range(H // 2):
            tile = slice(128 * m, 128 * m + 128)
            first, second = swap_halves(orep[array, 2 * m], orep[array, 2 * m + 1])
            ref[0, :, tile] = first
            ref[1, :, tile] = second


COPIES = 180


def shards(query_proj, key_proj, value_proj, grad_output):
    row_count = query_proj.shape[0] * lax.axis_size("row")
    factor = 1.0 / math.sqrt(D // H * row_count)
    vmem = pl.BlockSpec(memory_space=pltpu.VMEM)
    blocks = pl.pallas_call(
        functools.partial(kernel, factor),
        out_shape=jax.ShapeDtypeStruct((4, H, C, 128), BF),
        in_specs=[vmem] * 4,
        out_specs=vmem,
        scratch_shapes=[
            pltpu.VMEM((4, H, C, 128), BF),
            pltpu.SemaphoreType.DMA((COPIES,)),
            pltpu.SemaphoreType.DMA((COPIES,)),
            *Unit.scratch(NZ, C),
            *Unit.scratch(NX, 2 * C),
        ],
        compiler_params=pltpu.CompilerParams(
            collective_id=0, has_side_effects=True, vmem_limit_bytes=48 * 2**20
        ),
        cost_estimate=pl.CostEstimate(flops=1_208_000_000, bytes_accessed=1_600_000, transcendentals=50_000),
        name="exchange_and_compute",
    )(query_proj, key_proj, value_proj, grad_output)
    return pl.pallas_call(
        repack,
        out_shape=(jax.ShapeDtypeStruct(query_proj.shape, BF),) * 4,
        in_specs=[vmem],
        out_specs=(vmem,) * 4,
        name="repack",
    )(blocks)


def solution(mesh):
    placed = P("row", "col", None)
    return jax.shard_map(
        shards,
        mesh=mesh,
        in_specs=(placed,) * 4,
        out_specs=(placed,) * 4,
        check_vma=False,
    )
```

```python
import functools
import math

import jax
import jax.numpy as jnp
from jax import lax
from jax.experimental import pallas as pl
from jax.experimental.pallas import tpu as pltpu
from jax.sharding import PartitionSpec as P

D = 768
H = 12
NX = 4
NZ = 8
C = 64
W = 512
J = 512
MESH = pl.DeviceIdType.MESH
BF = jnp.bfloat16
F32 = jnp.float32

ATTENDED, GRAD_QUERY, GRAD_KEY, GRAD_VALUE = range(4)


def swap_halves(first, second):
    half = first.shape[-1] // 2
    low = jnp.concatenate([first[:, :half], second[:, :half]], axis=1)
    high = jnp.concatenate([first[:, half:], second[:, half:]], axis=1)
    return low, high


def nt_dot(a, b):
    return lax.dot_general(a, b, (((1,), (1,)), ((), ())), preferred_element_type=F32)


def tn_dot(a, b):
    return lax.dot_general(a, b, (((0,), (0,)), ((), ())), preferred_element_type=F32)


class Unit:
    def __init__(self, net, n, cb, me, right, left, refs):
        self.net, self.n, self.cb, self.me = net, n, cb, me
        self.right, self.left = right, left
        (
            self.kv, self.qg, self.part, self.core_in, self.half, self.ylo_in, self.stat, self.stat_in,
            self.probs, self.mine, self.eacc, self.edge, self.edge_in, self.rterm, self.rsend,
            self.rrecv, self.fin,
        ) = refs
        self.ours = pl.ds(pl.multiple_of(net.yhi * cb, cb), cb)
        self.theirs = pl.ds(pl.multiple_of((1 - net.yhi) * cb, cb), cb)
        self.own = pl.ds(self.block(0), cb)
        self.quarter = cb // 2
        self.rows_q = pl.ds(
            pl.multiple_of(net.core * cb + net.ylo * self.quarter, self.quarter), self.quarter
        )
        self.ring, self.swap, self.core_copy, self.ylo_copy = {}, {}, {}, {}
        self.stat_copy, self.probs_copy, self.edge_copy, self.sums = {}, {}, {}, {}
        self.arrive, self.leave = {}, {}

    @staticmethod
    def scratch(n, cb):
        return [
            pltpu.VMEM((2, J, W), BF),
            pltpu.VMEM((2, 2 * cb, W), BF),
            pltpu.VMEM((2, 2 * cb, J), F32),
            pltpu.VMEM((2, cb, J), F32),
            pltpu.VMEM((2, cb, J), F32),
            pltpu.VMEM((2, cb // 2, J), F32),
            pltpu.VMEM((2, cb // 2, 128), F32),
            pltpu.VMEM((2, cb // 2, 128), F32),
            pltpu.VMEM((2, 2 * cb, J), BF),
            pltpu.VMEM((2, cb // 2, J), F32),
            pltpu.VMEM((2, 2 * cb, W), F32),
            pltpu.VMEM((2, cb, W), BF),
            pltpu.VMEM((2, cb, W), BF),
            pltpu.VMEM((2, J, W), F32),
            pltpu.VMEM((2, 2, n // 2, cb, W), BF),
            pltpu.VMEM((2, 2, n // 2, cb, W), BF),
            pltpu.VMEM((4, cb, W), BF),
        ]

    def block(self, offset):
        return pl.multiple_of(lax.rem(self.me + offset + self.n, self.n) * self.cb, self.cb)

    def ring_send(self, t, step):
        full = step < self.n // 2
        size = self.cb if full else self.cb // 2
        left_block = self.block(step - 1)
        there = self.kv.at[t, pl.ds(self.block(1 - step), size)]
        back = self.kv.at[t, pl.ds(left_block if full else left_block + self.cb // 2, size)]
        self.ring[t, step] = (
            self.net.remote(there, there, self.right),
            self.net.remote(back, back, self.left),
        )

    def ring_step(self, t, step):
        for copy in self.ring[t, step]:
            copy.wait_recv()
        if step < self.n // 2:
            self.ring_send(t, step + 1)

    def swap_start(self, t):
        mine = self.qg.at[t, self.ours]
        self.swap[t] = self.net.remote(mine, mine, self.net.partner)

    def swap_wait(self, t):
        copy = self.swap.pop(t, None)
        if copy is not None:
            copy.wait_recv()

    def s_compute(self, t):
        self.swap_wait(t)
        self.part[t] = nt_dot(self.qg[t], self.kv[t])
        other = pl.ds(pl.multiple_of((1 - self.net.core) * self.cb, self.cb), self.cb)
        self.core_copy[t] = self.net.remote(
            self.part.at[t, other], self.core_in.at[t], self.net.core_peer
        )

    def s_core(self, t):
        self.core_copy[t].wait_recv()
        rows = pl.ds(pl.multiple_of(self.net.core * self.cb, self.cb), self.cb)
        self.half[t] = self.part[t, rows] + self.core_in[t]
        other = pl.ds(
            pl.multiple_of((1 - self.net.ylo) * self.quarter, self.quarter), self.quarter
        )
        self.ylo_copy[t] = self.net.remote(
            self.half.at[t, other], self.ylo_in.at[t], self.net.ylo_peer
        )

    def s_reduce(self, t):
        self.ylo_copy[t].wait_recv()
        rows = pl.ds(pl.multiple_of(self.net.ylo * self.quarter, self.quarter), self.quarter)
        total = self.half[t, rows] + self.ylo_in[t]
        if t == 0:
            score = total * self.net.factor
            top = jnp.max(score, axis=1, keepdims=True)
            weight = jnp.exp(score - top)
            self.mine[0] = weight
            lane = lax.broadcasted_iota(jnp.int32, (self.quarter, 128), 1)
            self.stat[0] = jnp.where(lane == 0, top, jnp.sum(weight, axis=1, keepdims=True))
        else:
            self.mine[1] = total
            dot = jnp.sum(self.mine[0] * total, axis=1, keepdims=True)
            self.stat[1] = jnp.broadcast_to(dot, (self.quarter, 128))
        self.stat_copy[t] = self.net.remote(
            self.stat.at[t], self.stat_in.at[t], self.net.partner
        )

    def p_compute(self, t):
        self.stat_copy[t].wait_recv()
        here, there = self.stat[t], self.stat_in[t]
        if t == 0:
            top_a, top_b = here[:, 0:1], there[:, 0:1]
            top = jnp.maximum(top_a, top_b)
            scale_a, scale_b = jnp.exp(top_a - top), jnp.exp(top_b - top)
            total = here[:, 1:2] * scale_a + there[:, 1:2] * scale_b
            weights = self.mine[0] * (scale_a / total)
            self.mine[0] = weights
            self.probs[0, self.rows_q] = weights.astype(BF)
        else:
            row_dot = here[:, 0:1] + there[:, 0:1]
            self.probs[1, self.rows_q] = (
                self.net.factor * self.mine[0] * (self.mine[1] - row_dot)
            ).astype(BF)
        block = self.probs.at[t, self.rows_q]
        self.probs_copy[t] = [
            self.net.remote(block, block, peer)
            for peer in (self.net.ylo_peer, self.net.core_peer)
        ]

    def p_forward(self, t):
        for copy in self.probs_copy[t]:
            copy.wait_recv()
        start = self.net.core * self.cb + (1 - self.net.ylo) * self.quarter
        block = self.probs.at[t, pl.ds(pl.multiple_of(start, self.quarter), self.quarter)]
        self.probs_copy[t] = [self.net.remote(block, block, self.net.core_peer)]

    def out_compute(self, t):
        for copy in self.probs_copy[t]:
            copy.wait_recv()
        self.swap_wait(1 - t)
        self.rterm[t] = tn_dot(self.probs[t], self.qg[1 - t])
        self.rs_send(t, 1)

    def edge_start(self, t):
        self.eacc[t] = jnp.dot(self.probs[t], self.kv[1 - t], preferred_element_type=F32)
        self.edge[t] = self.eacc[t, self.theirs].astype(BF)
        self.edge_copy[t] = self.net.remote(
            self.edge.at[t], self.edge_in.at[t], self.net.partner
        )

    def rs_send(self, t, step):
        cb, half = self.cb, self.cb // 2
        for way, peer in ((0, self.right), (1, self.left)):
            start = self.block((self.n // 2 + 1 - step) * (1 if way == 0 else -1))
            first, rest = slice(half * way, half * way + half), slice(half - half * way, cb - half * way)
            send = self.rsend.at[t, way, step - 1]
            recv = self.rrecv.at[t, way, step - 1]
            if step == 1:
                send[first] = self.rterm[t, pl.ds(start + half * way, half)].astype(BF)
                send, recv = (ref.at[pl.ds(half * way, half)] for ref in (send, recv))
            else:
                self.sums[t, step - 1][way].wait_recv()
                arrived = self.rrecv.at[t, way, step - 2]
                if step == 2:
                    send[first] = (
                        self.rterm[t, pl.ds(start + half * way, half)] + arrived[first].astype(F32)
                    ).astype(BF)
                    send[rest] = self.rterm[t, pl.ds(start + half - half * way, half)].astype(BF)
                else:
                    send[...] = (
                        self.rterm[t, pl.ds(start, cb)] + arrived[...].astype(F32)
                    ).astype(BF)
            self.sums.setdefault((t, step), []).append(self.net.remote(send, recv, peer))

    def rs_end(self, t):
        last = self.n // 2
        for copy in self.sums[t, last]:
            copy.wait_recv()
        index = (GRAD_VALUE, GRAD_KEY)[t]
        self.fin[index] = (
            self.rterm[t, self.own]
            + (self.rrecv[t, 0, last - 1].astype(F32) + self.rrecv[t, 1, last - 1].astype(F32))
        ).astype(BF)
        self.out_send(index)

    def edge_end(self, t):
        self.edge_copy[t].wait_recv()
        index = (ATTENDED, GRAD_QUERY)[t]
        self.fin[index] = (
            self.eacc[t, self.ours] + self.edge_in[t].astype(F32)
        ).astype(BF)
        self.out_send(index)


class XUnit(Unit):
    def in_send(self, name, t):
        net = self.net
        lanes = net.lanes(net.x)
        array, ref, rows = (
            (t, self.kv, self.own) if name == 0 else (2 + t, self.qg, self.ours)
        )
        self.arrive[name, t] = [
            net.remote(net.rep.at[array, NZ + net.xs[k]], ref.at[t, rows, lanes], net.x_peers[k])
            for k in (2, 1, 3)
        ]
        ref[t, rows, lanes] = net.rep[array, NZ + net.x]

    def in_wait(self, name, t):
        for copy in self.arrive[name, t]:
            copy.wait_recv()

    def out_send(self, index):
        net = self.net
        self.leave[index] = [
            net.remote(
                self.fin.at[index, :, net.lanes(net.xs[k])], net.orep.at[index, NZ + net.x], net.x_peers[k]
            )
            for k in (2, 1, 3)
        ]
        net.orep[index, NZ + net.x] = self.fin[index, :, net.lanes(net.x)]

    def out_wait(self, index):
        for copy in self.leave[index]:
            copy.wait_recv()


class ZUnit(Unit):
    def in_send(self, name, t):
        net = self.net
        lanes = net.lanes(net.x)
        slot = net.x * 2 + lax.rem(net.z, 2)
        sub = lax.rem(net.z, 2) * C
        base = net.take(NZ)
        array, ref = (t, self.kv) if name == 0 else (2 + t, self.qg)
        for k in (4, 3, 5, 2, 6, 1, 7, 0):
            z_to = lax.rem(net.z + k, NZ)
            x_to = lax.rem(net.z // 2 + z_to, NX)
            start = (net.yhi if name else x_to) * self.cb + sub
            net.remote(
                net.rep.at[array, z_to],
                ref.at[t, pl.ds(pl.multiple_of(start, C), C), lanes],
                net.device(x=x_to, z=z_to),
                recv=base + slot, alone=None if k else x_to == net.x,
            )
        self.arrive[name, t] = [
            (ref.at[t, pl.ds(0, C), pl.ds(0, 128)], base + k) for k in range(NZ)
        ]

    def in_wait(self, name, t):
        for ref, index in self.arrive[name, t]:
            self.net.wait_recv(ref, index)

    def out_send(self, index):
        net = self.net
        pair = lax.rem(net.x - net.z + NZ, NX)
        base = net.take(NZ)
        for k in (2, 1, 3, 0):
            for s in range(2):
                z_to = pair * 2 + s
                net.remote(
                    self.fin.at[index, pl.ds(s * C, C), net.lanes(net.xs[k])],
                    net.orep.at[index, net.z],
                    net.device(x=net.xs[k], z=z_to),
                    recv=base + net.z, alone=None if k else z_to == net.z,
                )
        self.leave[index] = [(net.orep.at[index, k], base + k) for k in range(NZ)]

    def out_wait(self, index):
        for ref, slot in self.leave[index]:
            self.net.wait_recv(ref, slot)


class Net:
    def __init__(self, factor, rep, orep, send_sems, recv_sems):
        self.factor, self.rep, self.orep = factor, rep, orep
        self.send_sems, self.recv_sems = send_sems, recv_sems
        row, col = lax.axis_index("row"), lax.axis_index("col")
        self.ylo, self.x, self.core = row // 8, lax.rem(row // 2, NX), lax.rem(row, 2)
        self.z, self.yhi = col // 2, lax.rem(col, 2)
        self.xs = [lax.rem(self.x + k, NX) for k in range(NX)]
        self.x_peers = [self.device(x=x) for x in self.xs]
        self.partner = self.device(yhi=1 - self.yhi)
        self.core_peer = self.device(core=1 - self.core)
        self.ylo_peer = self.device(ylo=1 - self.ylo)
        self.sent, self.received, self.started = 0, 0, []

    def device(self, **at):
        ylo, x, core, z, yhi = (at.get(k, getattr(self, k)) for k in ("ylo", "x", "core", "z", "yhi"))
        return (ylo * 8 + x * 2 + core, z * 2 + yhi)

    def lanes(self, x):
        return pl.ds(pl.multiple_of(x * 128, 128), 128)

    def take(self, n):
        self.received += n
        return self.received - n

    def remote(self, src, dst, peer, recv=None, alone=None):
        recv = self.take(1) if recv is None else recv
        send = self.send_sems.at[self.sent]
        self.sent += 1
        copy = pltpu.make_async_remote_copy(
            src_ref=src, dst_ref=dst, send_sem=send, recv_sem=self.recv_sems.at[recv],
            device_id=peer, device_id_type=MESH,
        )
        if alone is None:
            copy.start()
        else:
            pl.when(jnp.logical_not(alone))(copy.start)
            pl.when(alone)(pltpu.make_async_copy(src, dst, self.recv_sems.at[recv]).start)
        self.started.append((copy, alone))
        return copy

    def wait_recv(self, ref, index):
        pltpu.make_async_copy(ref, ref, self.recv_sems.at[index]).wait()

    def finish(self):
        for copy, alone in self.started:
            if alone is None:
                copy.wait_send()
            else:
                pl.when(jnp.logical_not(alone))(copy.wait_send)


def kernel(factor, q_ref, k_ref, v_ref, g_ref, a_out, gq_out, gk_out, gv_out, *refs):
    staged, results, rep, orep, send_sems, recv_sems, local_sems, *refs = refs
    net = Net(factor, rep, orep, send_sems, recv_sems)
    count = len(refs) // 2
    small = XUnit(
        net, NZ, C, net.z,
        net.device(z=lax.rem(net.z + 1, NZ)), net.device(z=lax.rem(net.z + NZ - 1, NZ)), refs[:count],
    )
    big = ZUnit(net, NX, 2 * C, net.x, net.x_peers[1], net.x_peers[3], refs[count:])

    order = ((0, k_ref), (2, q_ref), (1, v_ref), (3, g_ref))
    fetches = {}
    for array, ref in order:
        fetches[array] = pltpu.make_async_copy(ref, staged.at[array], local_sems.at[array])
        fetches[array].start()

    barrier = pltpu.get_barrier_semaphore()

    def greet(peer):
        pl.semaphore_signal(barrier, inc=1, device_id=peer, device_id_type=MESH)

    near = net.x_peers[1:] + [small.right, small.left, net.partner, net.core_peer, net.ylo_peer]
    pair = lax.rem(net.x - net.z + NZ, NX)
    for k in (2, 1, 3, 0):
        for s in range(2):
            peer = net.device(x=net.xs[k], z=pair * 2 + s)
            if k:
                greet(peer)
            else:
                pl.when(pair * 2 + s != net.z)(functools.partial(greet, peer))
    for peer in near:
        greet(peer)

    for array, _ in order:
        fetches[array].wait()
        for m in range(H // 2):
            tile = slice(128 * m, 128 * m + 128)
            low, high = swap_halves(staged[array, 0, :, tile], staged[array, 1, :, tile])
            rep[array, 2 * m] = low
            rep[array, 2 * m + 1] = high

    alone = (lax.rem(net.z // 2 + net.z, NX) == net.x).astype(jnp.int32)
    pl.semaphore_wait(barrier, len(near) + NZ - alone)

    def ring_start(unit, t):
        unit.in_wait(0, t)
        unit.ring_send(t, 1)

    def swap_start(unit, t):
        unit.in_wait(1, t)
        unit.swap_start(t)

    small.in_send(0, 0)
    big.in_send(0, 0)
    ring_start(small, 0)
    big.in_send(1, 0)
    small.in_send(1, 0)
    small.in_send(0, 1)
    small.ring_step(0, 1)
    ring_start(big, 0)
    ring_start(small, 1)
    small.ring_step(0, 2)
    small.in_send(1, 1)
    swap_start(big, 0)
    big.ring_step(0, 1)
    small.ring_step(1, 1)
    big.in_send(0, 1)
    swap_start(small, 1)
    swap_start(small, 0)
    small.ring_step(0, 3)
    big.ring_step(0, 2)
    big.in_send(1, 1)
    big.s_compute(0)
    small.ring_step(1, 2)
    small.ring_step(0, 4)
    big.s_core(0)
    ring_start(big, 1)
    small.s_compute(0)
    small.s_core(0)
    small.ring_step(1, 3)
    swap_start(big, 1)
    small.s_reduce(0)
    small.ring_step(1, 4)
    small.s_compute(1)
    big.ring_step(1, 1)
    big.s_reduce(0)
    small.s_core(1)
    small.p_compute(0)
    big.ring_step(1, 2)
    big.s_compute(1)
    big.p_compute(0)
    small.s_reduce(1)
    big.s_core(1)
    small.p_forward(0)
    small.out_compute(0)
    small.p_compute(1)
    big.p_forward(0)
    small.rs_send(0, 2)
    big.s_reduce(1)
    big.out_compute(0)
    big.edge_start(0)
    small.p_forward(1)
    small.out_compute(1)
    small.rs_send(0, 3)
    big.rs_send(0, 2)
    big.p_compute(1)
    small.rs_send(1, 2)
    big.edge_end(0)
    big.p_forward(1)
    small.rs_send(1, 3)
    big.out_compute(1)
    big.edge_start(1)
    big.rs_end(0)
    small.rs_send(1, 4)
    big.rs_send(1, 2)
    small.edge_start(1)
    small.rs_send(0, 4)
    big.edge_end(1)
    small.rs_end(1)
    small.edge_start(0)
    small.edge_end(1)
    small.rs_end(0)
    big.rs_end(1)
    small.edge_end(0)

    stores = []
    for index, ref in ((0, a_out), (1, gq_out), (3, gv_out), (2, gk_out)):
        big.out_wait(index)
        small.out_wait(index)
        for m in range(H // 2):
            tile = slice(128 * m, 128 * m + 128)
            first, second = swap_halves(orep[index, 2 * m], orep[index, 2 * m + 1])
            results[index, 0, :, tile] = first
            results[index, 1, :, tile] = second
        stores.append(pltpu.make_async_copy(results.at[index], ref, local_sems.at[4 + index]))
        stores[-1].start()
    net.finish()
    for copy in stores:
        copy.wait()


def hand_over(*refs):
    sources, targets, held, sems = refs[:4], refs[4:8], refs[8], refs[9]
    reads = [pltpu.make_async_copy(sources[i], held.at[i], sems.at[i]) for i in range(4)]
    writes = [pltpu.make_async_copy(held.at[i], targets[i], sems.at[4 + i]) for i in range(4)]
    for copy in reads:
        copy.start()
    for read, write in zip(reads, writes):
        read.wait()
        write.start()
    for copy in writes:
        copy.wait()


COPIES = 180


def shards(query_proj, key_proj, value_proj, grad_output):
    row_count = query_proj.shape[0] * lax.axis_size("row")
    factor = 1.0 / math.sqrt(D // H * row_count)
    anywhere = pl.BlockSpec(memory_space=pl.ANY)
    shape = query_proj.shape
    results = pl.pallas_call(
        functools.partial(kernel, factor),
        out_shape=(jax.ShapeDtypeStruct(shape, BF),) * 4,
        in_specs=[anywhere] * 4,
        out_specs=(anywhere,) * 4,
        scratch_shapes=[
            pltpu.VMEM((4, *shape), BF),
            pltpu.VMEM((4, *shape), BF),
            pltpu.VMEM((4, H, C, 128), BF),
            pltpu.VMEM((4, H, C, 128), BF),
            pltpu.SemaphoreType.DMA((COPIES,)),
            pltpu.SemaphoreType.DMA((COPIES,)),
            pltpu.SemaphoreType.DMA((8,)),
            *Unit.scratch(NZ, C),
            *Unit.scratch(NX, 2 * C),
        ],
        compiler_params=pltpu.CompilerParams(
            collective_id=0, has_side_effects=True, vmem_limit_bytes=60 * 2**20
        ),
        cost_estimate=pl.CostEstimate(flops=1_208_000_000, bytes_accessed=1_600_000, transcendentals=50_000),
        name="exchange_and_compute",
    )(query_proj, key_proj, value_proj, grad_output)
    return pl.pallas_call(
        hand_over,
        out_shape=(jax.ShapeDtypeStruct(shape, BF),) * 4,
        in_specs=[anywhere] * 4,
        out_specs=(anywhere,) * 4,
        scratch_shapes=[pltpu.VMEM((4, *shape), BF), pltpu.SemaphoreType.DMA((8,))],
        name="hand_over",
    )(*results)


def solution(mesh):
    placed = P("row", "col", None)
    return jax.shard_map(
        shards,
        mesh=mesh,
        in_specs=(placed,) * 4,
        out_specs=(placed,) * 4,
        check_vma=False,
    )
```

```python
import functools
import math

import jax
import jax.numpy as jnp
from jax import lax
from jax.experimental import pallas as pl
from jax.experimental.pallas import tpu as pltpu
from jax.sharding import PartitionSpec as P

D = 768
H = 12
NX = 4
NZ = 8
C = 64
W = 512
J = 512
POOL_MAX, POOL_STEP = 2**20, 2**14
MESH = pl.DeviceIdType.MESH
BF = jnp.bfloat16
F32 = jnp.float32

ATTENDED, GRAD_QUERY, GRAD_KEY, GRAD_VALUE = range(4)


def swap_halves(first, second):
    half = first.shape[-1] // 2
    low = jnp.concatenate([first[:, :half], second[:, :half]], axis=1)
    high = jnp.concatenate([first[:, half:], second[:, half:]], axis=1)
    return low, high


def nt_dot(a, b):
    return lax.dot_general(a, b, (((1,), (1,)), ((), ())), preferred_element_type=F32)


def tn_dot(a, b):
    return lax.dot_general(a, b, (((0,), (0,)), ((), ())), preferred_element_type=F32)


class Unit:
    def __init__(self, net, n, cb, me, right, left, whole, refs):
        self.net, self.n, self.cb, self.me = net, n, cb, me
        self.whole = whole
        self.right, self.left = right, left
        (
            self.kv, self.qg, self.part, self.core_in, self.half, self.ylo_in, self.stat, self.stat_in,
            self.probs, self.mine, self.eacc, self.edge, self.edge_in, self.rterm, self.rsend,
            self.rrecv, self.fin,
        ) = refs
        self.ours = pl.ds(pl.multiple_of(net.yhi * cb, cb), cb)
        self.theirs = pl.ds(pl.multiple_of((1 - net.yhi) * cb, cb), cb)
        self.own = pl.ds(self.block(0), cb)
        self.quarter = cb if whole else cb // 2
        self.part_of_half = 0 if whole else net.ylo
        self.rows_q = pl.ds(
            pl.multiple_of(net.core * cb + self.part_of_half * self.quarter, self.quarter), self.quarter
        )
        self.ring, self.swap, self.core_copy, self.ylo_copy = {}, {}, {}, {}
        self.stat_copy, self.probs_copy, self.edge_copy, self.sums = {}, {}, {}, {}
        self.arrive, self.leave = {}, {}

    @staticmethod
    def scratch(n, cb, whole):
        quarter = cb if whole else cb // 2
        return [
            pltpu.VMEM((2, J, W), BF),
            pltpu.VMEM((2, 2 * cb, W), BF),
            pltpu.VMEM((2, 2 * cb, J), F32),
            pltpu.VMEM((2, cb, J), F32),
            pltpu.VMEM((2, cb, J), F32),
            pltpu.VMEM((2, quarter, J), F32),
            pltpu.VMEM((2, 8, 128), F32),
            pltpu.VMEM((2, 8, 128), F32),
            pltpu.VMEM((2, 2 * cb, J), BF),
            pltpu.VMEM((2, quarter, J), F32),
            pltpu.VMEM((2, 2 * cb, W), F32),
            pltpu.VMEM((2, cb, W), BF),
            pltpu.VMEM((2, cb, W), BF),
            pltpu.VMEM((2, J, W), F32),
            pltpu.VMEM((2, 2, n // 2, cb, W), BF),
            pltpu.VMEM((2, 2, n // 2, cb, W), BF),
            pltpu.VMEM((4, cb, W), BF),
        ]

    def block(self, offset):
        return pl.multiple_of(lax.rem(self.me + offset + self.n, self.n) * self.cb, self.cb)

    def ring_send(self, t, step):
        full = step < self.n // 2
        size = self.cb if full else self.cb // 2
        left_block = self.block(step - 1)
        there = self.kv.at[t, pl.ds(self.block(1 - step), size)]
        back = self.kv.at[t, pl.ds(left_block if full else left_block + self.cb // 2, size)]
        recv = self.net.remote(there, there, self.right)
        self.ring[t, step] = self.net.remote(back, back, self.left, recv=recv)

    def ring_step(self, t, step):
        size = 2 * self.cb if step < self.n // 2 else self.cb
        self.net.wait_recv(self.kv.at[t, pl.ds(0, size)], self.ring[t, step])
        if step < self.n // 2:
            self.ring_send(t, step + 1)

    def swap_start(self, t):
        mine = self.qg.at[t, self.ours]
        self.swap[t] = self.net.remote(mine, mine, self.net.partner)

    def swap_wait(self, t):
        recv = self.swap.pop(t, None)
        if recv is not None:
            self.net.wait_recv(self.qg.at[t, self.theirs], recv)

    def s_compute(self, t):
        self.swap_wait(t)
        self.part[t] = nt_dot(self.qg[t], self.kv[t])
        other = pl.ds(pl.multiple_of((1 - self.net.core) * self.cb, self.cb), self.cb)
        self.core_copy[t] = self.net.remote(
            self.part.at[t, other], self.core_in.at[t], self.net.core_peer
        )

    def s_core(self, t):
        self.net.wait_recv(self.core_in.at[t], self.core_copy[t])
        rows = pl.ds(pl.multiple_of(self.net.core * self.cb, self.cb), self.cb)
        self.half[t] = self.part[t, rows] + self.core_in[t]
        start = 0 if self.whole else (1 - self.net.ylo) * self.quarter
        other = pl.ds(pl.multiple_of(start, self.quarter), self.quarter)
        self.ylo_copy[t] = self.net.remote(
            self.half.at[t, other], self.ylo_in.at[t], self.net.ylo_peer
        )

    def s_reduce(self, t):
        self.net.wait_recv(self.ylo_in.at[t], self.ylo_copy[t])
        rows = pl.ds(pl.multiple_of(self.part_of_half * self.quarter, self.quarter), self.quarter)
        total = self.half[t, rows] + self.ylo_in[t]
        if t == 0:
            score = total * self.net.factor
            top = jnp.max(score, axis=1, keepdims=True)
            weight = jnp.exp(score - top)
            self.mine[0] = weight
            self.stat[0] = self.to_rows(top, jnp.sum(weight, axis=1, keepdims=True))
        else:
            self.mine[1] = total
            dot = jnp.sum(self.mine[0] * total, axis=1, keepdims=True)
            self.stat[1] = self.to_rows(dot, dot)
        self.stat_copy[t] = self.net.remote(
            self.stat.at[t], self.stat_in.at[t], self.net.partner
        )

    def to_rows(self, first, second):
        lane = lax.broadcasted_iota(jnp.int32, (self.quarter, 128), 1)
        wide = jnp.where(lane == 0, first, second)
        wide = jnp.concatenate([wide] * (128 // self.quarter), axis=0)
        return wide.T[:8]

    def to_columns(self, rows):
        wide = jnp.concatenate([rows] * 16, axis=0).T[: self.quarter]
        return wide[:, 0:1], wide[:, 1:2]

    def p_compute(self, t):
        self.net.wait_recv(self.stat_in.at[t], self.stat_copy[t])
        top_a, total_a = self.to_columns(self.stat[t])
        top_b, total_b = self.to_columns(self.stat_in[t])
        if t == 0:
            top = jnp.maximum(top_a, top_b)
            scale_a, scale_b = jnp.exp(top_a - top), jnp.exp(top_b - top)
            total = total_a * scale_a + total_b * scale_b
            weights = self.mine[0] * (scale_a / total)
            self.mine[0] = weights
            self.probs[0, self.rows_q] = weights.astype(BF)
        else:
            row_dot = top_a + top_b
            self.probs[1, self.rows_q] = (
                self.net.factor * self.mine[0] * (self.mine[1] - row_dot)
            ).astype(BF)
        block = self.probs.at[t, self.rows_q]
        recv = None if self.whole else self.net.remote(block, block, self.net.ylo_peer)
        self.probs_copy[t] = self.net.remote(block, block, self.net.core_peer, recv=recv)

    def p_forward(self, t):
        arrived = self.probs.at[t, pl.ds(0, 2 * self.quarter)]
        self.net.wait_recv(arrived, self.probs_copy[t])
        start = self.net.core * self.cb + (1 - self.net.ylo) * self.quarter
        block = self.probs.at[t, pl.ds(pl.multiple_of(start, self.quarter), self.quarter)]
        self.probs_copy[t] = self.net.remote(block, block, self.net.core_peer)

    def out_compute(self, t):
        self.net.wait_recv(self.probs.at[t, pl.ds(0, self.quarter)], self.probs_copy[t])
        self.swap_wait(1 - t)
        self.rterm[t] = tn_dot(self.probs[t], self.qg[1 - t])
        self.rs_send(t, 1)

    def edge_start(self, t):
        self.eacc[t] = jnp.dot(self.probs[t], self.kv[1 - t], preferred_element_type=F32)
        self.edge[t] = self.eacc[t, self.theirs].astype(BF)
        self.edge_copy[t] = self.net.remote(
            self.edge.at[t], self.edge_in.at[t], self.net.partner
        )

    def rs_send(self, t, step):
        cb, half = self.cb, self.cb // 2
        if step > 1:
            self.rs_wait(t, step - 1)
        recv = None
        for way, peer in ((0, self.right), (1, self.left)):
            start = self.block((self.n // 2 + 1 - step) * (1 if way == 0 else -1))
            first, rest = slice(half * way, half * way + half), slice(half - half * way, cb - half * way)
            send = self.rsend.at[t, way, step - 1]
            into = self.rrecv.at[t, way, step - 1]
            if step == 1:
                send[first] = self.rterm[t, pl.ds(start + half * way, half)].astype(BF)
                send, into = (ref.at[pl.ds(half * way, half)] for ref in (send, into))
            else:
                arrived = self.rrecv.at[t, way, step - 2]
                if step == 2:
                    send[first] = (
                        self.rterm[t, pl.ds(start + half * way, half)] + arrived[first].astype(F32)
                    ).astype(BF)
                    send[rest] = self.rterm[t, pl.ds(start + half - half * way, half)].astype(BF)
                else:
                    send[...] = (
                        self.rterm[t, pl.ds(start, cb)] + arrived[...].astype(F32)
                    ).astype(BF)
            recv = self.net.remote(send, into, peer, recv=recv)
        self.sums[t, step] = recv

    def rs_wait(self, t, step):
        size = self.cb // 2 if step == 1 else self.cb
        self.net.wait_recv(self.rrecv.at[t, :, step - 1, pl.ds(0, size)], self.sums[t, step])

    def rs_end(self, t):
        last = self.n // 2
        self.rs_wait(t, last)
        index = (GRAD_VALUE, GRAD_KEY)[t]
        self.fin[index] = (
            self.rterm[t, self.own]
            + (self.rrecv[t, 0, last - 1].astype(F32) + self.rrecv[t, 1, last - 1].astype(F32))
        ).astype(BF)
        self.out_send(index)

    def edge_end(self, t):
        self.net.wait_recv(self.edge_in.at[t], self.edge_copy[t])
        index = (ATTENDED, GRAD_QUERY)[t]
        self.fin[index] = (
            self.eacc[t, self.ours] + self.edge_in[t].astype(F32)
        ).astype(BF)
        self.out_send(index)


class XUnit(Unit):
    def in_send(self, name, t):
        net = self.net
        lanes = net.lanes(net.x)
        array, ref, rows = (
            (t, self.kv, self.own) if name == 0 else (2 + t, self.qg, self.ours)
        )
        recv = net.take()
        for k in (2, 1, 3):
            net.remote(
                net.rep.at[array, NZ + net.xs[k]], ref.at[t, rows, lanes], net.x_peers[k], recv=recv
            )
        self.arrive[name, t] = recv
        ref[t, rows, lanes] = net.rep[array, NZ + net.x]

    def in_wait(self, name, t):
        ref, rows = (self.kv, self.own) if name == 0 else (self.qg, self.ours)
        self.net.wait_recv(ref.at[t, rows, pl.ds(0, 3 * 128)], self.arrive[name, t])

    def out_send(self, index):
        net = self.net
        recv = net.take()
        for k in (2, 1, 3):
            net.remote(
                self.fin.at[index, :, net.lanes(net.xs[k])], net.orep.at[index, NZ + net.x],
                net.x_peers[k], recv=recv,
            )
        self.leave[index] = recv
        net.orep[index, NZ + net.x] = self.fin[index, :, net.lanes(net.x)]

    def out_wait(self, index):
        self.net.wait_recv(self.net.orep.at[index, pl.ds(NZ, 3)], self.leave[index])


class ZUnit(Unit):
    def in_send(self, name, t):
        net = self.net
        lanes = net.lanes(net.x)
        sub = lax.rem(net.z, 2) * C
        recv = net.take()
        array, ref = (t, self.kv) if name == 0 else (2 + t, self.qg)
        for k in (4, 3, 5, 2, 6, 1, 7, 0):
            z_to = lax.rem(net.z + k, NZ)
            x_to = lax.rem(net.z // 2 + z_to, NX)
            start = (net.yhi if name else x_to) * self.cb + sub
            net.remote(
                net.rep.at[array, z_to],
                ref.at[t, pl.ds(pl.multiple_of(start, C), C), lanes],
                net.device(x=x_to, z=z_to),
                recv=recv, alone=None if k else x_to == net.x, key="in",
            )
        self.arrive[name, t] = recv

    def in_wait(self, name, t):
        block = self.kv.at[t, self.own] if name == 0 else self.qg.at[t, self.ours]
        self.net.wait_recv(block, self.arrive[name, t])

    def out_send(self, index):
        net = self.net
        pair = lax.rem(net.x - net.z + NZ, NX)
        recv = net.take()
        for k in (2, 1, 3, 0):
            for s in range(2):
                z_to = pair * 2 + s
                net.remote(
                    self.fin.at[index, pl.ds(s * C, C), net.lanes(net.xs[k])],
                    net.orep.at[index, net.z],
                    net.device(x=net.xs[k], z=z_to),
                    recv=recv, alone=None if k else z_to == net.z, key=("out", s),
                )
        self.leave[index] = recv

    def out_wait(self, index):
        self.net.wait_recv(self.net.orep.at[index, pl.ds(0, NZ)], self.leave[index])


class Net:
    def __init__(self, factor, rep, orep, send_sems, recv_sems):
        self.factor, self.rep, self.orep = factor, rep, orep
        self.send_sems, self.recv_sems = send_sems, recv_sems
        row, col = lax.axis_index("row"), lax.axis_index("col")
        self.ylo, self.x, self.core = row // 8, lax.rem(row // 2, NX), lax.rem(row, 2)
        self.z, self.yhi = col // 2, lax.rem(col, 2)
        self.xs = [lax.rem(self.x + k, NX) for k in range(NX)]
        self.x_peers = [self.device(x=x) for x in self.xs]
        self.partner = self.device(yhi=1 - self.yhi)
        self.core_peer = self.device(core=1 - self.core)
        self.ylo_peer = self.device(ylo=1 - self.ylo)
        self.received, self.groups, self.pools = 0, [], {}

    def device(self, **at):
        ylo, x, core, z, yhi = (at.get(k, getattr(self, k)) for k in ("ylo", "x", "core", "z", "yhi"))
        return (ylo * 8 + x * 2 + core, z * 2 + yhi)

    def lanes(self, x):
        return pl.ds(pl.multiple_of(x * 128, 128), 128)

    def take(self):
        self.received += 1
        return self.received - 1

    def remote(self, src, dst, peer, recv=None, alone=None, key=None):
        recv = self.take() if recv is None else recv
        size = math.prod(src.shape) * src.dtype.itemsize
        if alone is None:
            name = "small" if size < POOL_STEP else "pool"
            group = self.pools.get(name)
            if group is None or group[1] + size > POOL_MAX:
                group = self.new_group(None)
                self.pools[name] = group
        else:
            group = self.pools.get(key) or self.new_group(alone)
            self.pools[key] = group
        group[1] += size
        copy = pltpu.make_async_remote_copy(
            src_ref=src, dst_ref=dst, send_sem=self.send_sems.at[group[0]],
            recv_sem=self.recv_sems.at[recv], device_id=peer, device_id_type=MESH,
        )
        if alone is None:
            copy.start()
        else:
            pl.when(jnp.logical_not(alone))(copy.start)
            pl.when(alone)(pltpu.make_async_copy(src, dst, self.recv_sems.at[recv]).start)
        return recv

    def new_group(self, alone):
        self.groups.append([len(self.groups), 0, alone])
        return self.groups[-1]

    def wait_recv(self, ref, index):
        pltpu.make_async_copy(ref, ref, self.recv_sems.at[index]).wait()

    def finish(self, ref):
        for index, size, alone in self.groups:
            view = ref.at[pl.ds(0, size // 2048)]
            copy = pltpu.make_async_remote_copy(
                src_ref=view, dst_ref=view, send_sem=self.send_sems.at[index],
                recv_sem=self.recv_sems.at[0], device_id=self.partner, device_id_type=MESH,
            )
            if alone is None:
                copy.wait_send()
            else:
                pl.when(jnp.logical_not(alone))(copy.wait_send)


def kernel(factor, q_ref, k_ref, v_ref, g_ref, a_out, gq_out, gk_out, gv_out, *refs):
    staged, results, rep, orep, send_sems, recv_sems, local_sems, *refs = refs
    net = Net(factor, rep, orep, send_sems, recv_sems)
    count = len(refs) // 2
    small = XUnit(
        net, NZ, C, net.z,
        net.device(z=lax.rem(net.z + 1, NZ)), net.device(z=lax.rem(net.z + NZ - 1, NZ)), True, refs[:count],
    )
    big = ZUnit(net, NX, 2 * C, net.x, net.x_peers[1], net.x_peers[3], False, refs[count:])

    order = ((0, k_ref), (2, q_ref), (1, v_ref), (3, g_ref))
    fetches = {}
    for array, ref in order:
        fetches[array] = pltpu.make_async_copy(ref, staged.at[array], local_sems.at[array])
        fetches[array].start()

    barrier = pltpu.get_barrier_semaphore()

    def greet(peer):
        pl.semaphore_signal(barrier, inc=1, device_id=peer, device_id_type=MESH)

    near = net.x_peers[1:] + [small.right, small.left, net.partner, net.core_peer, net.ylo_peer]
    pair = lax.rem(net.x - net.z + NZ, NX)
    for k in (2, 1, 3, 0):
        for s in range(2):
            peer = net.device(x=net.xs[k], z=pair * 2 + s)
            if k:
                greet(peer)
            else:
                pl.when(pair * 2 + s != net.z)(functools.partial(greet, peer))
    for peer in near:
        greet(peer)

    for array, _ in order:
        fetches[array].wait()
        for m in range(H // 2):
            tile = slice(128 * m, 128 * m + 128)
            low, high = swap_halves(staged[array, 0, :, tile], staged[array, 1, :, tile])
            rep[array, 2 * m] = low
            rep[array, 2 * m + 1] = high

    alone = (lax.rem(net.z // 2 + net.z, NX) == net.x).astype(jnp.int32)
    pl.semaphore_wait(barrier, len(near) + NZ - alone)

    def ring_start(unit, t):
        unit.in_wait(0, t)
        unit.ring_send(t, 1)

    def swap_start(unit, t):
        unit.in_wait(1, t)
        unit.swap_start(t)

    big.in_send(0, 0)
    small.in_send(1, 0)
    small.in_send(0, 0)
    big.in_send(1, 0)
    small.in_send(0, 1)
    ring_start(small, 0)
    ring_start(big, 0)
    ring_start(small, 1)
    small.ring_step(0, 1)
    small.in_send(1, 1)
    big.in_send(0, 1)
    swap_start(big, 0)
    big.ring_step(0, 1)
    swap_start(small, 0)
    swap_start(small, 1)
    small.ring_step(0, 2)
    small.ring_step(1, 1)
    big.ring_step(0, 2)
    big.s_compute(0)
    small.ring_step(0, 3)
    big.in_send(1, 1)
    big.s_core(0)
    small.ring_step(0, 4)
    small.s_compute(0)
    ring_start(big, 1)
    small.ring_step(1, 2)
    small.s_core(0)
    big.s_reduce(0)
    swap_start(big, 1)
    small.ring_step(1, 3)
    big.ring_step(1, 1)
    small.s_reduce(0)
    small.ring_step(1, 4)
    small.s_compute(1)
    big.p_compute(0)
    big.ring_step(1, 2)
    small.s_core(1)
    small.p_compute(0)
    big.s_compute(1)
    small.out_compute(0)
    big.p_forward(0)
    big.s_core(1)
    big.out_compute(0)
    small.rs_send(0, 2)
    small.s_reduce(1)
    big.rs_send(0, 2)
    small.rs_send(0, 3)
    big.s_reduce(1)
    small.p_compute(1)
    small.out_compute(1)
    big.p_compute(1)
    small.rs_send(0, 4)
    big.edge_start(0)
    small.rs_send(1, 2)
    big.rs_end(0)
    big.p_forward(1)
    small.rs_send(1, 3)
    big.out_compute(1)
    big.edge_start(1)
    small.edge_start(0)
    big.edge_end(0)
    big.rs_send(1, 2)
    small.rs_send(1, 4)
    small.edge_start(1)
    big.edge_end(1)
    big.rs_end(1)
    small.rs_end(1)
    small.edge_end(1)
    small.edge_end(0)
    small.rs_end(0)

    stores = []
    for index, ref in ((0, a_out), (1, gq_out), (3, gv_out), (2, gk_out)):
        big.out_wait(index)
        small.out_wait(index)
        for m in range(H // 2):
            tile = slice(128 * m, 128 * m + 128)
            first, second = swap_halves(orep[index, 2 * m], orep[index, 2 * m + 1])
            results[index, 0, :, tile] = first
            results[index, 1, :, tile] = second
        stores.append(pltpu.make_async_copy(results.at[index], ref, local_sems.at[4 + index]))
        stores[-1].start()
    net.finish(small.rterm.at[0])
    for copy in stores:
        copy.wait()


def hand_over(*refs):
    sources, targets, held, sems = refs[:4], refs[4:8], refs[8], refs[9]
    reads = [pltpu.make_async_copy(sources[i], held.at[i], sems.at[i]) for i in range(4)]
    writes = [pltpu.make_async_copy(held.at[i], targets[i], sems.at[4 + i]) for i in range(4)]
    for copy in reads:
        copy.start()
    for read, write in zip(reads, writes):
        read.wait()
        write.start()
    for copy in writes:
        copy.wait()


SENDS, RECEIVES = 12, 66


def shards(query_proj, key_proj, value_proj, grad_output):
    row_count = query_proj.shape[0] * lax.axis_size("row")
    factor = 1.0 / math.sqrt(D // H * row_count)
    anywhere = pl.BlockSpec(memory_space=pl.ANY)
    shape = query_proj.shape
    results = pl.pallas_call(
        functools.partial(kernel, factor),
        out_shape=(jax.ShapeDtypeStruct(shape, BF),) * 4,
        in_specs=[anywhere] * 4,
        out_specs=(anywhere,) * 4,
        scratch_shapes=[
            pltpu.VMEM((4, *shape), BF),
            pltpu.VMEM((4, *shape), BF),
            pltpu.VMEM((4, H, C, 128), BF),
            pltpu.VMEM((4, H, C, 128), BF),
            pltpu.SemaphoreType.DMA((SENDS,)),
            pltpu.SemaphoreType.DMA((RECEIVES,)),
            pltpu.SemaphoreType.DMA((8,)),
            *Unit.scratch(NZ, C, True),
            *Unit.scratch(NX, 2 * C, False),
        ],
        compiler_params=pltpu.CompilerParams(
            collective_id=0, has_side_effects=True, vmem_limit_bytes=60 * 2**20
        ),
        cost_estimate=pl.CostEstimate(flops=1_208_000_000, bytes_accessed=1_600_000, transcendentals=50_000),
        name="exchange_and_compute",
    )(query_proj, key_proj, value_proj, grad_output)
    return pl.pallas_call(
        hand_over,
        out_shape=(jax.ShapeDtypeStruct(shape, BF),) * 4,
        in_specs=[anywhere] * 4,
        out_specs=(anywhere,) * 4,
        scratch_shapes=[pltpu.VMEM((4, *shape), BF), pltpu.SemaphoreType.DMA((8,))],
        name="hand_over",
    )(*results)


def solution(mesh):
    placed = P("row", "col", None)
    return jax.shard_map(
        shards,
        mesh=mesh,
        in_specs=(placed,) * 4,
        out_specs=(placed,) * 4,
        check_vma=False,
    )
```

```python
import functools
import math

import jax
import jax.numpy as jnp
from jax import lax
from jax.experimental import pallas as pl
from jax.experimental.pallas import tpu as pltpu
from jax.sharding import PartitionSpec as P

D = 768
H = 12
NX = 4
NZ = 8
C = 64
W = 512
J = 512
POOL_MAX, POOL_STEP = 2**20, 2**14
MESH = pl.DeviceIdType.MESH
BF = jnp.bfloat16
F32 = jnp.float32

ATTENDED, GRAD_QUERY, GRAD_KEY, GRAD_VALUE = range(4)


def swap_halves(first, second):
    half = first.shape[-1] // 2
    low = jnp.concatenate([first[:, :half], second[:, :half]], axis=1)
    high = jnp.concatenate([first[:, half:], second[:, half:]], axis=1)
    return low, high


def nt_dot(a, b):
    return lax.dot_general(a, b, (((1,), (1,)), ((), ())), preferred_element_type=F32)


def tn_dot(a, b):
    return lax.dot_general(a, b, (((0,), (0,)), ((), ())), preferred_element_type=F32)


class Unit:
    def __init__(self, net, n, cb, me, right, left, whole, refs):
        self.net, self.n, self.cb, self.me = net, n, cb, me
        self.whole = whole
        self.right, self.left = right, left
        (
            self.kv, self.qg, self.part, self.core_in, self.half, self.ylo_in, self.stat, self.stat_in,
            self.probs, self.mine, self.eacc, self.edge, self.edge_in, self.rterm, self.rsend,
            self.rrecv, self.fin,
        ) = refs
        self.ours = pl.ds(pl.multiple_of(net.yhi * cb, cb), cb)
        self.theirs = pl.ds(pl.multiple_of((1 - net.yhi) * cb, cb), cb)
        self.own = pl.ds(self.block(0), cb)
        self.quarter = cb if whole else cb // 2
        self.part_of_half = 0 if whole else net.ylo
        self.rows_q = pl.ds(
            pl.multiple_of(net.core * cb + self.part_of_half * self.quarter, self.quarter), self.quarter
        )
        self.ring, self.swap, self.core_copy, self.ylo_copy = {}, {}, {}, {}
        self.stat_copy, self.probs_copy, self.edge_copy, self.sums = {}, {}, {}, {}
        self.arrive, self.leave = {}, {}

    @staticmethod
    def scratch(n, cb, whole):
        quarter = cb if whole else cb // 2
        return [
            pltpu.VMEM((2, J, W), BF),
            pltpu.VMEM((2, 2 * cb, W), BF),
            pltpu.VMEM((2, 2 * cb, J), F32),
            pltpu.VMEM((2, cb, J), F32),
            pltpu.VMEM((2, cb, J), F32),
            pltpu.VMEM((2, quarter, J), F32),
            pltpu.VMEM((2, 8, 128), F32),
            pltpu.VMEM((2, 8, 128), F32),
            pltpu.VMEM((2, 2 * cb, J), BF),
            pltpu.VMEM((2, quarter, J), F32),
            pltpu.VMEM((2, 2 * cb, W), F32),
            pltpu.VMEM((2, cb, W), BF),
            pltpu.VMEM((2, cb, W), BF),
            pltpu.VMEM((2, J, W), F32),
            pltpu.VMEM((2, 2, n // 2, cb, W), BF),
            pltpu.VMEM((2, 2, n // 2, cb, W), BF),
            pltpu.VMEM((4, cb, W), BF),
        ]

    def block(self, offset):
        return pl.multiple_of(lax.rem(self.me + offset + self.n, self.n) * self.cb, self.cb)

    def ring_send(self, t, step):
        full = step < self.n // 2
        size = self.cb if full else self.cb // 2
        left_block = self.block(step - 1)
        there = self.kv.at[t, pl.ds(self.block(1 - step), size)]
        back = self.kv.at[t, pl.ds(left_block if full else left_block + self.cb // 2, size)]
        recv = self.net.remote(there, there, self.right)
        self.ring[t, step] = self.net.remote(back, back, self.left, recv=recv)

    def ring_step(self, t, step):
        size = 2 * self.cb if step < self.n // 2 else self.cb
        self.net.wait_recv(self.kv.at[t, pl.ds(0, size)], self.ring[t, step])
        if step < self.n // 2:
            self.ring_send(t, step + 1)

    def swap_start(self, t):
        mine = self.qg.at[t, self.ours]
        self.swap[t] = self.net.remote(mine, mine, self.net.partner)

    def swap_wait(self, t):
        recv = self.swap.pop(t, None)
        if recv is not None:
            self.net.wait_recv(self.qg.at[t, self.theirs], recv)

    def s_compute(self, t):
        self.swap_wait(t)
        self.part[t] = nt_dot(self.qg[t], self.kv[t])
        other = pl.ds(pl.multiple_of((1 - self.net.core) * self.cb, self.cb), self.cb)
        self.core_copy[t] = self.net.remote(
            self.part.at[t, other], self.core_in.at[t], self.net.core_peer
        )

    def s_core(self, t):
        self.net.wait_recv(self.core_in.at[t], self.core_copy[t])
        rows = pl.ds(pl.multiple_of(self.net.core * self.cb, self.cb), self.cb)
        self.half[t] = self.part[t, rows] + self.core_in[t]
        start = 0 if self.whole else (1 - self.net.ylo) * self.quarter
        other = pl.ds(pl.multiple_of(start, self.quarter), self.quarter)
        self.ylo_copy[t] = self.net.remote(
            self.half.at[t, other], self.ylo_in.at[t], self.net.ylo_peer
        )

    def s_reduce(self, t):
        self.net.wait_recv(self.ylo_in.at[t], self.ylo_copy[t])
        rows = pl.ds(pl.multiple_of(self.part_of_half * self.quarter, self.quarter), self.quarter)
        total = self.half[t, rows] + self.ylo_in[t]
        if t == 0:
            score = total * self.net.factor
            top = jnp.max(score, axis=1, keepdims=True)
            weight = jnp.exp(score - top)
            self.mine[0] = weight
            self.stat[0] = self.to_rows(top, jnp.sum(weight, axis=1, keepdims=True))
        else:
            self.mine[1] = total
            dot = jnp.sum(self.mine[0] * total, axis=1, keepdims=True)
            self.stat[1] = self.to_rows(dot, dot)
        self.stat_copy[t] = self.net.remote(
            self.stat.at[t], self.stat_in.at[t], self.net.partner
        )

    def to_rows(self, first, second):
        lane = lax.broadcasted_iota(jnp.int32, (self.quarter, 128), 1)
        wide = jnp.where(lane == 0, first, second)
        wide = jnp.concatenate([wide] * (128 // self.quarter), axis=0)
        return wide.T[:8]

    def to_columns(self, rows):
        wide = jnp.concatenate([rows] * 16, axis=0).T[: self.quarter]
        return wide[:, 0:1], wide[:, 1:2]

    def p_compute(self, t):
        self.net.wait_recv(self.stat_in.at[t], self.stat_copy[t])
        top_a, total_a = self.to_columns(self.stat[t])
        top_b, total_b = self.to_columns(self.stat_in[t])
        if t == 0:
            top = jnp.maximum(top_a, top_b)
            scale_a, scale_b = jnp.exp(top_a - top), jnp.exp(top_b - top)
            total = total_a * scale_a + total_b * scale_b
            weights = self.mine[0] * (scale_a / total)
            self.mine[0] = weights
            self.probs[0, self.rows_q] = weights.astype(BF)
        else:
            row_dot = top_a + top_b
            self.probs[1, self.rows_q] = (
                self.net.factor * self.mine[0] * (self.mine[1] - row_dot)
            ).astype(BF)
        block = self.probs.at[t, self.rows_q]
        recv = None if self.whole else self.net.remote(block, block, self.net.ylo_peer)
        self.probs_copy[t] = self.net.remote(block, block, self.net.core_peer, recv=recv)

    def p_forward(self, t):
        arrived = self.probs.at[t, pl.ds(0, 2 * self.quarter)]
        self.net.wait_recv(arrived, self.probs_copy[t])
        start = self.net.core * self.cb + (1 - self.net.ylo) * self.quarter
        block = self.probs.at[t, pl.ds(pl.multiple_of(start, self.quarter), self.quarter)]
        self.probs_copy[t] = self.net.remote(block, block, self.net.core_peer)

    def out_compute(self, t):
        self.net.wait_recv(self.probs.at[t, pl.ds(0, self.quarter)], self.probs_copy[t])
        self.swap_wait(1 - t)
        self.rterm[t] = tn_dot(self.probs[t], self.qg[1 - t])
        self.rs_send(t, 1)

    def edge_start(self, t):
        self.eacc[t] = jnp.dot(self.probs[t], self.kv[1 - t], preferred_element_type=F32)
        self.edge[t] = self.eacc[t, self.theirs].astype(BF)
        self.edge_copy[t] = self.net.remote(
            self.edge.at[t], self.edge_in.at[t], self.net.partner
        )

    def rs_send(self, t, step):
        cb, half = self.cb, self.cb // 2
        if step > 1:
            self.rs_wait(t, step - 1)
        recv = None
        for way, peer in ((0, self.right), (1, self.left)):
            start = self.block((self.n // 2 + 1 - step) * (1 if way == 0 else -1))
            first, rest = slice(half * way, half * way + half), slice(half - half * way, cb - half * way)
            send = self.rsend.at[t, way, step - 1]
            into = self.rrecv.at[t, way, step - 1]
            if step == 1:
                send[first] = self.rterm[t, pl.ds(start + half * way, half)].astype(BF)
                send, into = (ref.at[pl.ds(half * way, half)] for ref in (send, into))
            else:
                arrived = self.rrecv.at[t, way, step - 2]
                if step == 2:
                    send[first] = (
                        self.rterm[t, pl.ds(start + half * way, half)] + arrived[first].astype(F32)
                    ).astype(BF)
                    send[rest] = self.rterm[t, pl.ds(start + half - half * way, half)].astype(BF)
                else:
                    send[...] = (
                        self.rterm[t, pl.ds(start, cb)] + arrived[...].astype(F32)
                    ).astype(BF)
            recv = self.net.remote(send, into, peer, recv=recv)
        self.sums[t, step] = recv

    def rs_wait(self, t, step):
        size = self.cb // 2 if step == 1 else self.cb
        self.net.wait_recv(self.rrecv.at[t, :, step - 1, pl.ds(0, size)], self.sums[t, step])

    def rs_end(self, t):
        last = self.n // 2
        self.rs_wait(t, last)
        index = (GRAD_VALUE, GRAD_KEY)[t]
        self.fin[index] = (
            self.rterm[t, self.own]
            + (self.rrecv[t, 0, last - 1].astype(F32) + self.rrecv[t, 1, last - 1].astype(F32))
        ).astype(BF)
        self.out_send(index)

    def edge_end(self, t):
        self.net.wait_recv(self.edge_in.at[t], self.edge_copy[t])
        index = (ATTENDED, GRAD_QUERY)[t]
        self.fin[index] = (
            self.eacc[t, self.ours] + self.edge_in[t].astype(F32)
        ).astype(BF)
        self.out_send(index)


class XUnit(Unit):
    def in_send(self, name, t):
        net = self.net
        lanes = net.lanes(net.x)
        array, ref, rows = (
            (t, self.kv, self.own) if name == 0 else (2 + t, self.qg, self.ours)
        )
        recv = net.take()
        for k in (2, 1, 3):
            net.remote(
                net.rep.at[array, NZ + net.xs[k]], ref.at[t, rows, lanes], net.x_peers[k], recv=recv
            )
        self.arrive[name, t] = recv
        ref[t, rows, lanes] = net.rep[array, NZ + net.x]

    def in_wait(self, name, t):
        ref, rows = (self.kv, self.own) if name == 0 else (self.qg, self.ours)
        self.net.wait_recv(ref.at[t, rows, pl.ds(0, 3 * 128)], self.arrive[name, t])

    def out_send(self, index):
        net = self.net
        recv = net.take()
        for k in (2, 1, 3):
            net.remote(
                self.fin.at[index, :, net.lanes(net.xs[k])], net.orep.at[index, NZ + net.x],
                net.x_peers[k], recv=recv,
            )
        self.leave[index] = recv
        net.orep[index, NZ + net.x] = self.fin[index, :, net.lanes(net.x)]

    def out_wait(self, index):
        self.net.wait_recv(self.net.orep.at[index, pl.ds(NZ, 3)], self.leave[index])


class ZUnit(Unit):
    def in_send(self, name, t):
        net = self.net
        lanes = net.lanes(net.x)
        sub = lax.rem(net.z, 2) * C
        recv = net.take()
        array, ref = (t, self.kv) if name == 0 else (2 + t, self.qg)
        for k in (4, 3, 5, 2, 6, 1, 7, 0):
            z_to = lax.rem(net.z + k, NZ)
            x_to = lax.rem(net.z // 2 + z_to, NX)
            start = (net.yhi if name else x_to) * self.cb + sub
            net.remote(
                net.rep.at[array, z_to],
                ref.at[t, pl.ds(pl.multiple_of(start, C), C), lanes],
                net.device(x=x_to, z=z_to),
                recv=recv, alone=None if k else x_to == net.x, key="in",
            )
        self.arrive[name, t] = recv

    def in_wait(self, name, t):
        block = self.kv.at[t, self.own] if name == 0 else self.qg.at[t, self.ours]
        self.net.wait_recv(block, self.arrive[name, t])

    def out_send(self, index):
        net = self.net
        pair = lax.rem(net.x - net.z + NZ, NX)
        recv = net.take()
        for k in (2, 1, 3, 0):
            for s in range(2):
                z_to = pair * 2 + s
                net.remote(
                    self.fin.at[index, pl.ds(s * C, C), net.lanes(net.xs[k])],
                    net.orep.at[index, net.z],
                    net.device(x=net.xs[k], z=z_to),
                    recv=recv, alone=None if k else z_to == net.z, key=("out", s),
                )
        self.leave[index] = recv

    def out_wait(self, index):
        self.net.wait_recv(self.net.orep.at[index, pl.ds(0, NZ)], self.leave[index])


class Net:
    def __init__(self, factor, rep, orep, send_sems, recv_sems):
        self.factor, self.rep, self.orep = factor, rep, orep
        self.send_sems, self.recv_sems = send_sems, recv_sems
        row, col = lax.axis_index("row"), lax.axis_index("col")
        self.ylo, self.x, self.core = row // 8, lax.rem(row // 2, NX), lax.rem(row, 2)
        self.z, self.yhi = col // 2, lax.rem(col, 2)
        self.xs = [lax.rem(self.x + k, NX) for k in range(NX)]
        self.x_peers = [self.device(x=x) for x in self.xs]
        self.partner = self.device(yhi=1 - self.yhi)
        self.core_peer = self.device(core=1 - self.core)
        self.ylo_peer = self.device(ylo=1 - self.ylo)
        self.received, self.groups, self.pools = 0, [], {}

    def device(self, **at):
        ylo, x, core, z, yhi = (at.get(k, getattr(self, k)) for k in ("ylo", "x", "core", "z", "yhi"))
        return (ylo * 8 + x * 2 + core, z * 2 + yhi)

    def lanes(self, x):
        return pl.ds(pl.multiple_of(x * 128, 128), 128)

    def take(self):
        self.received += 1
        return self.received - 1

    def remote(self, src, dst, peer, recv=None, alone=None, key=None):
        recv = self.take() if recv is None else recv
        size = math.prod(src.shape) * src.dtype.itemsize
        if alone is None:
            name = "small" if size < POOL_STEP else "pool"
            group = self.pools.get(name)
            if group is None or group[1] + size > POOL_MAX:
                group = self.new_group(None)
                self.pools[name] = group
        else:
            group = self.pools.get(key) or self.new_group(alone)
            self.pools[key] = group
        group[1] += size
        copy = pltpu.make_async_remote_copy(
            src_ref=src, dst_ref=dst, send_sem=self.send_sems.at[group[0]],
            recv_sem=self.recv_sems.at[recv], device_id=peer, device_id_type=MESH,
        )
        if alone is None:
            copy.start()
        else:
            pl.when(jnp.logical_not(alone))(copy.start)
            pl.when(alone)(pltpu.make_async_copy(src, dst, self.recv_sems.at[recv]).start)
        return recv

    def new_group(self, alone):
        self.groups.append([len(self.groups), 0, alone])
        return self.groups[-1]

    def wait_recv(self, ref, index):
        pltpu.make_async_copy(ref, ref, self.recv_sems.at[index]).wait()

    def finish(self, ref):
        for index, size, alone in self.groups:
            view = ref.at[pl.ds(0, size // 2048)]
            copy = pltpu.make_async_remote_copy(
                src_ref=view, dst_ref=view, send_sem=self.send_sems.at[index],
                recv_sem=self.recv_sems.at[0], device_id=self.partner, device_id_type=MESH,
            )
            if alone is None:
                copy.wait_send()
            else:
                pl.when(jnp.logical_not(alone))(copy.wait_send)


def kernel(factor, q_ref, k_ref, v_ref, g_ref, a_out, gq_out, gk_out, gv_out, *refs):
    staged, results, rep, orep, send_sems, recv_sems, local_sems, *refs = refs
    net = Net(factor, rep, orep, send_sems, recv_sems)
    count = len(refs) // 2
    small = XUnit(
        net, NZ, C, net.z,
        net.device(z=lax.rem(net.z + 1, NZ)), net.device(z=lax.rem(net.z + NZ - 1, NZ)), True, refs[:count],
    )
    big = ZUnit(net, NX, 2 * C, net.x, net.x_peers[1], net.x_peers[3], False, refs[count:])

    order = ((0, k_ref), (2, q_ref), (1, v_ref), (3, g_ref))
    fetches = {}
    for array, ref in order:
        fetches[array] = pltpu.make_async_copy(ref, staged.at[array], local_sems.at[array])
        fetches[array].start()

    barrier = pltpu.get_barrier_semaphore()

    def greet(peer):
        pl.semaphore_signal(barrier, inc=1, device_id=peer, device_id_type=MESH)

    near = net.x_peers[1:] + [small.right, small.left, net.partner, net.core_peer, net.ylo_peer]
    pair = lax.rem(net.x - net.z + NZ, NX)
    for k in (2, 1, 3, 0):
        for s in range(2):
            peer = net.device(x=net.xs[k], z=pair * 2 + s)
            if k:
                greet(peer)
            else:
                pl.when(pair * 2 + s != net.z)(functools.partial(greet, peer))
    for peer in near:
        greet(peer)

    def prepare(array):
        fetches.pop(array).wait()
        for m in range(H // 2):
            tile = slice(128 * m, 128 * m + 128)
            low, high = swap_halves(staged[array, 0, :, tile], staged[array, 1, :, tile])
            rep[array, 2 * m] = low
            rep[array, 2 * m + 1] = high

    def in_send(unit, name, t):
        if 2 * name + t in fetches:
            prepare(2 * name + t)
        unit.in_send(name, t)

    prepare(0)
    alone = (lax.rem(net.z // 2 + net.z, NX) == net.x).astype(jnp.int32)
    pl.semaphore_wait(barrier, len(near) + NZ - alone)

    def ring_start(unit, t):
        unit.in_wait(0, t)
        unit.ring_send(t, 1)

    def swap_start(unit, t):
        unit.in_wait(1, t)
        unit.swap_start(t)

    in_send(big, 0, 0)
    in_send(small, 0, 0)
    in_send(small, 1, 0)
    in_send(big, 1, 0)
    in_send(small, 0, 1)
    ring_start(small, 0)
    ring_start(big, 0)
    ring_start(small, 1)
    small.ring_step(0, 1)
    in_send(small, 1, 1)
    in_send(big, 0, 1)
    swap_start(big, 0)
    big.ring_step(0, 1)
    swap_start(small, 0)
    small.ring_step(0, 2)
    small.ring_step(1, 1)
    swap_start(small, 1)
    big.ring_step(0, 2)
    big.s_compute(0)
    ring_start(big, 1)
    small.ring_step(0, 3)
    in_send(big, 1, 1)
    big.s_core(0)
    small.ring_step(0, 4)
    small.s_compute(0)
    small.ring_step(1, 2)
    small.s_core(0)
    big.s_reduce(0)
    swap_start(big, 1)
    small.ring_step(1, 3)
    big.ring_step(1, 1)
    small.s_reduce(0)
    small.ring_step(1, 4)
    small.s_compute(1)
    big.p_compute(0)
    big.ring_step(1, 2)
    small.s_core(1)
    small.p_compute(0)
    big.s_compute(1)
    small.out_compute(0)
    big.p_forward(0)
    big.s_core(1)
    big.out_compute(0)
    small.rs_send(0, 2)
    small.s_reduce(1)
    big.rs_send(0, 2)
    small.rs_send(0, 3)
    big.s_reduce(1)
    small.p_compute(1)
    small.out_compute(1)
    big.p_compute(1)
    small.rs_send(0, 4)
    big.edge_start(0)
    small.rs_send(1, 2)
    big.rs_end(0)
    big.p_forward(1)
    small.rs_send(1, 3)
    big.out_compute(1)
    big.edge_start(1)
    small.edge_start(0)
    big.edge_end(0)
    big.rs_send(1, 2)
    small.rs_send(1, 4)
    small.edge_start(1)
    big.edge_end(1)
    big.rs_end(1)
    small.rs_end(1)
    small.edge_end(1)
    small.edge_end(0)
    small.rs_end(0)

    stores = []
    for index, ref in ((0, a_out), (1, gq_out), (3, gv_out), (2, gk_out)):
        big.out_wait(index)
        small.out_wait(index)
        for m in range(H // 2):
            tile = slice(128 * m, 128 * m + 128)
            first, second = swap_halves(orep[index, 2 * m], orep[index, 2 * m + 1])
            results[index, 0, :, tile] = first
            results[index, 1, :, tile] = second
        stores.append(pltpu.make_async_copy(results.at[index], ref, local_sems.at[4 + index]))
        stores[-1].start()
    net.finish(small.rterm.at[0])
    for copy in stores:
        copy.wait()


def hand_over(*refs):
    sources, targets, held, sems = refs[:4], refs[4:8], refs[8], refs[9]
    reads = [pltpu.make_async_copy(sources[i], held.at[i], sems.at[i]) for i in range(4)]
    writes = [pltpu.make_async_copy(held.at[i], targets[i], sems.at[4 + i]) for i in range(4)]
    for copy in reads:
        copy.start()
    for read, write in zip(reads, writes):
        read.wait()
        write.start()
    for copy in writes:
        copy.wait()


SENDS, RECEIVES = 12, 66


def shards(query_proj, key_proj, value_proj, grad_output):
    row_count = query_proj.shape[0] * lax.axis_size("row")
    factor = 1.0 / math.sqrt(D // H * row_count)
    anywhere = pl.BlockSpec(memory_space=pl.ANY)
    shape = query_proj.shape
    results = pl.pallas_call(
        functools.partial(kernel, factor),
        out_shape=(jax.ShapeDtypeStruct(shape, BF),) * 4,
        in_specs=[anywhere] * 4,
        out_specs=(anywhere,) * 4,
        scratch_shapes=[
            pltpu.VMEM((4, *shape), BF),
            pltpu.VMEM((4, *shape), BF),
            pltpu.VMEM((4, H, C, 128), BF),
            pltpu.VMEM((4, H, C, 128), BF),
            pltpu.SemaphoreType.DMA((SENDS,)),
            pltpu.SemaphoreType.DMA((RECEIVES,)),
            pltpu.SemaphoreType.DMA((8,)),
            *Unit.scratch(NZ, C, True),
            *Unit.scratch(NX, 2 * C, False),
        ],
        compiler_params=pltpu.CompilerParams(
            collective_id=0, has_side_effects=True, vmem_limit_bytes=60 * 2**20
        ),
        cost_estimate=pl.CostEstimate(flops=1_208_000_000, bytes_accessed=1_600_000, transcendentals=50_000),
        name="exchange_and_compute",
    )(query_proj, key_proj, value_proj, grad_output)
    return pl.pallas_call(
        hand_over,
        out_shape=(jax.ShapeDtypeStruct(shape, BF),) * 4,
        in_specs=[anywhere] * 4,
        out_specs=(anywhere,) * 4,
        scratch_shapes=[pltpu.VMEM((4, *shape), BF), pltpu.SemaphoreType.DMA((8,))],
        name="hand_over",
    )(*results)


def solution(mesh):
    placed = P("row", "col", None)
    return jax.shard_map(
        shards,
        mesh=mesh,
        in_specs=(placed,) * 4,
        out_specs=(placed,) * 4,
        check_vma=False,
    )
```

```python
import functools
import math

import jax
import jax.numpy as jnp
from jax import lax
from jax.experimental import pallas as pl
from jax.experimental.pallas import tpu as pltpu
from jax.sharding import PartitionSpec as P

D = 768
H = 12
NX = 4
NZ = 8
C = 64
W = 512
J = 512
POOL_MAX, POOL_STEP = 2**20, 2**14
MESH = pl.DeviceIdType.MESH
BF = jnp.bfloat16
F32 = jnp.float32

ATTENDED, GRAD_QUERY, GRAD_KEY, GRAD_VALUE = range(4)


def swap_halves(first, second):
    half = first.shape[-1] // 2
    low = jnp.concatenate([first[:, :half], second[:, :half]], axis=1)
    high = jnp.concatenate([first[:, half:], second[:, half:]], axis=1)
    return low, high


def nt_dot(a, b):
    return lax.dot_general(a, b, (((1,), (1,)), ((), ())), preferred_element_type=F32)


def tn_dot(a, b):
    return lax.dot_general(a, b, (((0,), (0,)), ((), ())), preferred_element_type=F32)


class Unit:
    def __init__(self, net, n, cb, me, right, left, whole, refs):
        self.net, self.n, self.cb, self.me = net, n, cb, me
        self.whole = whole
        self.right, self.left = right, left
        (
            self.kv, self.qg, self.part, self.core_in, self.half, self.ylo_in, self.stat, self.stat_in,
            self.probs, self.mine, self.eacc, self.edge, self.edge_in, self.rterm, self.rsend,
            self.rrecv, self.fin,
        ) = refs
        self.ours = pl.ds(pl.multiple_of(net.yhi * cb, cb), cb)
        self.theirs = pl.ds(pl.multiple_of((1 - net.yhi) * cb, cb), cb)
        self.own = pl.ds(self.block(0), cb)
        self.quarter = cb if whole else cb // 2
        self.part_of_half = 0 if whole else net.ylo
        self.rows_q = pl.ds(
            pl.multiple_of(net.core * cb + self.part_of_half * self.quarter, self.quarter), self.quarter
        )
        self.ring, self.swap, self.core_copy, self.ylo_copy = {}, {}, {}, {}
        self.stat_copy, self.probs_copy, self.edge_copy, self.sums = {}, {}, {}, {}
        self.arrive, self.leave = {}, {}

    @staticmethod
    def scratch(n, cb, whole):
        quarter = cb if whole else cb // 2
        return [
            pltpu.VMEM((2, J, W), BF),
            pltpu.VMEM((2, 2 * cb, W), BF),
            pltpu.VMEM((2, 2 * cb, J), F32),
            pltpu.VMEM((2, cb, J), F32),
            pltpu.VMEM((2, cb, J), F32),
            pltpu.VMEM((2, quarter, J), F32),
            pltpu.VMEM((2, 8, 128), F32),
            pltpu.VMEM((2, 8, 128), F32),
            pltpu.VMEM((2, 2 * cb, J), BF),
            pltpu.VMEM((2, quarter, J), F32),
            pltpu.VMEM((2, 2 * cb, W), F32),
            pltpu.VMEM((2, cb, W), BF),
            pltpu.VMEM((2, cb, W), BF),
            pltpu.VMEM((2, J, W), F32),
            pltpu.VMEM((2, 2, n // 2, cb, W), BF),
            pltpu.VMEM((2, 2, n // 2, cb, W), BF),
            pltpu.VMEM((4, cb, W), BF),
        ]

    def block(self, offset):
        return pl.multiple_of(lax.rem(self.me + offset + self.n, self.n) * self.cb, self.cb)

    def ring_send(self, t, step):
        full = step < self.n // 2
        size = self.cb if full else self.cb // 2
        left_block = self.block(step - 1)
        there = self.kv.at[t, pl.ds(self.block(1 - step), size)]
        back = self.kv.at[t, pl.ds(left_block if full else left_block + self.cb // 2, size)]
        recv = self.net.remote(there, there, self.right)
        self.ring[t, step] = self.net.remote(back, back, self.left, recv=recv)

    def ring_step(self, t, step):
        size = 2 * self.cb if step < self.n // 2 else self.cb
        self.net.wait_recv(self.kv.at[t, pl.ds(0, size)], self.ring[t, step])
        if step < self.n // 2:
            self.ring_send(t, step + 1)

    def swap_start(self, t):
        mine = self.qg.at[t, self.ours]
        self.swap[t] = self.net.remote(mine, mine, self.net.partner)

    def swap_wait(self, t):
        recv = self.swap.pop(t, None)
        if recv is not None:
            self.net.wait_recv(self.qg.at[t, self.theirs], recv)

    def s_compute(self, t):
        self.swap_wait(t)
        self.part[t] = nt_dot(self.qg[t], self.kv[t])
        other = pl.ds(pl.multiple_of((1 - self.net.core) * self.cb, self.cb), self.cb)
        self.core_copy[t] = self.net.remote(
            self.part.at[t, other], self.core_in.at[t], self.net.core_peer
        )

    def s_core(self, t):
        self.net.wait_recv(self.core_in.at[t], self.core_copy[t])
        rows = pl.ds(pl.multiple_of(self.net.core * self.cb, self.cb), self.cb)
        self.half[t] = self.part[t, rows] + self.core_in[t]
        start = 0 if self.whole else (1 - self.net.ylo) * self.quarter
        other = pl.ds(pl.multiple_of(start, self.quarter), self.quarter)
        self.ylo_copy[t] = self.net.remote(
            self.half.at[t, other], self.ylo_in.at[t], self.net.ylo_peer
        )

    def s_reduce(self, t):
        self.net.wait_recv(self.ylo_in.at[t], self.ylo_copy[t])
        rows = pl.ds(pl.multiple_of(self.part_of_half * self.quarter, self.quarter), self.quarter)
        total = self.half[t, rows] + self.ylo_in[t]
        if t == 0:
            score = total * self.net.factor
            top = jnp.max(score, axis=1, keepdims=True)
            weight = jnp.exp(score - top)
            self.mine[0] = weight
            self.stat[0] = self.to_rows(top, jnp.sum(weight, axis=1, keepdims=True))
        else:
            self.mine[1] = total
            dot = jnp.sum(self.mine[0] * total, axis=1, keepdims=True)
            self.stat[1] = self.to_rows(dot, dot)
        self.stat_copy[t] = self.net.remote(
            self.stat.at[t], self.stat_in.at[t], self.net.partner
        )

    def to_rows(self, first, second):
        lane = lax.broadcasted_iota(jnp.int32, (self.quarter, 128), 1)
        wide = jnp.where(lane == 0, first, second)
        wide = jnp.concatenate([wide] * (128 // self.quarter), axis=0)
        return wide.T[:8]

    def to_columns(self, rows):
        wide = jnp.concatenate([rows] * 16, axis=0).T[: self.quarter]
        return wide[:, 0:1], wide[:, 1:2]

    def p_compute(self, t):
        self.net.wait_recv(self.stat_in.at[t], self.stat_copy[t])
        top_a, total_a = self.to_columns(self.stat[t])
        top_b, total_b = self.to_columns(self.stat_in[t])
        if t == 0:
            top = jnp.maximum(top_a, top_b)
            scale_a, scale_b = jnp.exp(top_a - top), jnp.exp(top_b - top)
            total = total_a * scale_a + total_b * scale_b
            weights = self.mine[0] * (scale_a / total)
            self.mine[0] = weights
            self.probs[0, self.rows_q] = weights.astype(BF)
        else:
            row_dot = top_a + top_b
            self.probs[1, self.rows_q] = (
                self.net.factor * self.mine[0] * (self.mine[1] - row_dot)
            ).astype(BF)
        block = self.probs.at[t, self.rows_q]
        recv = None if self.whole else self.net.remote(block, block, self.net.ylo_peer)
        self.probs_copy[t] = self.net.remote(block, block, self.net.core_peer, recv=recv)

    def p_forward(self, t):
        arrived = self.probs.at[t, pl.ds(0, 2 * self.quarter)]
        self.net.wait_recv(arrived, self.probs_copy[t])
        start = self.net.core * self.cb + (1 - self.net.ylo) * self.quarter
        block = self.probs.at[t, pl.ds(pl.multiple_of(start, self.quarter), self.quarter)]
        self.probs_copy[t] = self.net.remote(block, block, self.net.core_peer)

    def out_compute(self, t):
        self.net.wait_recv(self.probs.at[t, pl.ds(0, self.quarter)], self.probs_copy[t])
        self.swap_wait(1 - t)
        self.rterm[t] = tn_dot(self.probs[t], self.qg[1 - t])
        self.rs_send(t, 1)

    def edge_start(self, t):
        self.eacc[t] = jnp.dot(self.probs[t], self.kv[1 - t], preferred_element_type=F32)
        self.edge[t] = self.eacc[t, self.theirs].astype(BF)
        self.edge_copy[t] = self.net.remote(
            self.edge.at[t], self.edge_in.at[t], self.net.partner
        )

    def rs_send(self, t, step):
        cb, half = self.cb, self.cb // 2
        if step > 1:
            self.rs_wait(t, step - 1)
        recv = None
        for way, peer in ((0, self.right), (1, self.left)):
            start = self.block((self.n // 2 + 1 - step) * (1 if way == 0 else -1))
            first, rest = slice(half * way, half * way + half), slice(half - half * way, cb - half * way)
            send = self.rsend.at[t, way, step - 1]
            into = self.rrecv.at[t, way, step - 1]
            if step == 1:
                send[first] = self.rterm[t, pl.ds(start + half * way, half)].astype(BF)
                send, into = (ref.at[pl.ds(half * way, half)] for ref in (send, into))
            else:
                arrived = self.rrecv.at[t, way, step - 2]
                if step == 2:
                    send[first] = (
                        self.rterm[t, pl.ds(start + half * way, half)] + arrived[first].astype(F32)
                    ).astype(BF)
                    send[rest] = self.rterm[t, pl.ds(start + half - half * way, half)].astype(BF)
                else:
                    send[...] = (
                        self.rterm[t, pl.ds(start, cb)] + arrived[...].astype(F32)
                    ).astype(BF)
            recv = self.net.remote(send, into, peer, recv=recv)
        self.sums[t, step] = recv

    def rs_wait(self, t, step):
        size = self.cb // 2 if step == 1 else self.cb
        self.net.wait_recv(self.rrecv.at[t, :, step - 1, pl.ds(0, size)], self.sums[t, step])

    def rs_end(self, t):
        last = self.n // 2
        self.rs_wait(t, last)
        index = (GRAD_VALUE, GRAD_KEY)[t]
        self.fin[index] = (
            self.rterm[t, self.own]
            + (self.rrecv[t, 0, last - 1].astype(F32) + self.rrecv[t, 1, last - 1].astype(F32))
        ).astype(BF)
        self.out_send(index)

    def edge_end(self, t):
        self.net.wait_recv(self.edge_in.at[t], self.edge_copy[t])
        index = (ATTENDED, GRAD_QUERY)[t]
        self.fin[index] = (
            self.eacc[t, self.ours] + self.edge_in[t].astype(F32)
        ).astype(BF)
        self.out_send(index)


class XUnit(Unit):
    def in_send(self, name, t):
        net = self.net
        lanes = net.lanes(net.x)
        array, ref, rows = (
            (t, self.kv, self.own) if name == 0 else (2 + t, self.qg, self.ours)
        )
        recv = net.take()
        for k in (2, 1, 3):
            net.remote(
                net.rep.at[array, NZ + net.xs[k]], ref.at[t, rows, lanes], net.x_peers[k], recv=recv
            )
        self.arrive[name, t] = recv
        ref[t, rows, lanes] = net.rep[array, NZ + net.x]

    def in_wait(self, name, t):
        ref, rows = (self.kv, self.own) if name == 0 else (self.qg, self.ours)
        self.net.wait_recv(ref.at[t, rows, pl.ds(0, 3 * 128)], self.arrive[name, t])

    def out_send(self, index):
        net = self.net
        recv = net.take()
        for k in (2, 1, 3):
            net.remote(
                self.fin.at[index, :, net.lanes(net.xs[k])], net.orep.at[index, NZ + net.x],
                net.x_peers[k], recv=recv,
            )
        self.leave[index] = recv
        net.orep[index, NZ + net.x] = self.fin[index, :, net.lanes(net.x)]

    def out_wait(self, index):
        self.net.wait_recv(self.net.orep.at[index, pl.ds(NZ, 3)], self.leave[index])


class ZUnit(Unit):
    def in_send(self, name, t):
        net = self.net
        lanes = net.lanes(net.x)
        sub = lax.rem(net.z, 2) * C
        recv = net.take()
        array, ref = (t, self.kv) if name == 0 else (2 + t, self.qg)
        for k in (4, 3, 5, 2, 6, 1, 7, 0):
            z_to = lax.rem(net.z + k, NZ)
            x_to = lax.rem(net.z // 2 + z_to, NX)
            start = (net.yhi if name else x_to) * self.cb + sub
            net.remote(
                net.rep.at[array, z_to],
                ref.at[t, pl.ds(pl.multiple_of(start, C), C), lanes],
                net.device(x=x_to, z=z_to),
                recv=recv, alone=None if k else x_to == net.x, key="in",
            )
        self.arrive[name, t] = recv

    def in_wait(self, name, t):
        block = self.kv.at[t, self.own] if name == 0 else self.qg.at[t, self.ours]
        self.net.wait_recv(block, self.arrive[name, t])

    def out_send(self, index):
        self.leave[index] = self.net.take()

    def out_part(self, index, part):
        net = self.net
        pair = lax.rem(net.x - net.z + NZ, NX)
        k = (2, 1, 3, 0)[part]
        for s in range(2):
            z_to = pair * 2 + s
            net.remote(
                self.fin.at[index, pl.ds(s * C, C), net.lanes(net.xs[k])],
                net.orep.at[index, net.z],
                net.device(x=net.xs[k], z=z_to),
                recv=self.leave[index], alone=None if k else z_to == net.z, key=("out", s),
            )

    def out_wait(self, index):
        self.net.wait_recv(self.net.orep.at[index, pl.ds(0, NZ)], self.leave[index])


class Net:
    def __init__(self, factor, rep, orep, send_sems, recv_sems):
        self.factor, self.rep, self.orep = factor, rep, orep
        self.send_sems, self.recv_sems = send_sems, recv_sems
        row, col = lax.axis_index("row"), lax.axis_index("col")
        self.ylo, self.x, self.core = row // 8, lax.rem(row // 2, NX), lax.rem(row, 2)
        self.z, self.yhi = col // 2, lax.rem(col, 2)
        self.xs = [lax.rem(self.x + k, NX) for k in range(NX)]
        self.x_peers = [self.device(x=x) for x in self.xs]
        self.partner = self.device(yhi=1 - self.yhi)
        self.core_peer = self.device(core=1 - self.core)
        self.ylo_peer = self.device(ylo=1 - self.ylo)
        self.received, self.groups, self.pools = 0, [], {}

    def device(self, **at):
        ylo, x, core, z, yhi = (at.get(k, getattr(self, k)) for k in ("ylo", "x", "core", "z", "yhi"))
        return (ylo * 8 + x * 2 + core, z * 2 + yhi)

    def lanes(self, x):
        return pl.ds(pl.multiple_of(x * 128, 128), 128)

    def take(self):
        self.received += 1
        return self.received - 1

    def remote(self, src, dst, peer, recv=None, alone=None, key=None):
        recv = self.take() if recv is None else recv
        size = math.prod(src.shape) * src.dtype.itemsize
        if alone is None:
            name = "small" if size < POOL_STEP else "pool"
            group = self.pools.get(name)
            if group is None or group[1] + size > POOL_MAX:
                group = self.new_group(None)
                self.pools[name] = group
        else:
            group = self.pools.get(key) or self.new_group(alone)
            self.pools[key] = group
        group[1] += size
        copy = pltpu.make_async_remote_copy(
            src_ref=src, dst_ref=dst, send_sem=self.send_sems.at[group[0]],
            recv_sem=self.recv_sems.at[recv], device_id=peer, device_id_type=MESH,
        )
        if alone is None:
            copy.start()
        else:
            pl.when(jnp.logical_not(alone))(copy.start)
            pl.when(alone)(pltpu.make_async_copy(src, dst, self.recv_sems.at[recv]).start)
        return recv

    def new_group(self, alone):
        self.groups.append([len(self.groups), 0, alone])
        return self.groups[-1]

    def wait_recv(self, ref, index):
        pltpu.make_async_copy(ref, ref, self.recv_sems.at[index]).wait()

    def finish(self, ref):
        for index, size, alone in self.groups:
            view = ref.at[pl.ds(0, size // 2048)]
            copy = pltpu.make_async_remote_copy(
                src_ref=view, dst_ref=view, send_sem=self.send_sems.at[index],
                recv_sem=self.recv_sems.at[0], device_id=self.partner, device_id_type=MESH,
            )
            if alone is None:
                copy.wait_send()
            else:
                pl.when(jnp.logical_not(alone))(copy.wait_send)


def kernel(factor, q_ref, k_ref, v_ref, g_ref, a_out, gq_out, gk_out, gv_out, *refs):
    staged, results, rep, orep, send_sems, recv_sems, local_sems, *refs = refs
    net = Net(factor, rep, orep, send_sems, recv_sems)
    count = len(refs) // 2
    small = XUnit(
        net, NZ, C, net.z,
        net.device(z=lax.rem(net.z + 1, NZ)), net.device(z=lax.rem(net.z + NZ - 1, NZ)), True, refs[:count],
    )
    big = ZUnit(net, NX, 2 * C, net.x, net.x_peers[1], net.x_peers[3], False, refs[count:])

    order = ((0, k_ref), (2, q_ref), (1, v_ref), (3, g_ref))
    fetches = {}
    for array, ref in order:
        fetches[array] = pltpu.make_async_copy(ref, staged.at[array], local_sems.at[array])
        fetches[array].start()

    barrier = pltpu.get_barrier_semaphore()

    def greet(peer):
        pl.semaphore_signal(barrier, inc=1, device_id=peer, device_id_type=MESH)

    near = net.x_peers[1:] + [small.right, small.left, net.partner, net.core_peer, net.ylo_peer]
    pair = lax.rem(net.x - net.z + NZ, NX)
    for k in (2, 1, 3, 0):
        for s in range(2):
            peer = net.device(x=net.xs[k], z=pair * 2 + s)
            if k:
                greet(peer)
            else:
                pl.when(pair * 2 + s != net.z)(functools.partial(greet, peer))
    for peer in near:
        greet(peer)

    def prepare(array):
        fetches.pop(array).wait()
        for m in range(H // 2):
            tile = slice(128 * m, 128 * m + 128)
            low, high = swap_halves(staged[array, 0, :, tile], staged[array, 1, :, tile])
            rep[array, 2 * m] = low
            rep[array, 2 * m + 1] = high

    def in_send(unit, name, t):
        if 2 * name + t in fetches:
            prepare(2 * name + t)
        unit.in_send(name, t)

    prepare(0)
    alone = (lax.rem(net.z // 2 + net.z, NX) == net.x).astype(jnp.int32)
    pl.semaphore_wait(barrier, len(near) + NZ - alone)

    def ring_start(unit, t):
        unit.in_wait(0, t)
        unit.ring_send(t, 1)

    def swap_start(unit, t):
        unit.in_wait(1, t)
        unit.swap_start(t)

    in_send(big, 0, 0)
    in_send(small, 0, 0)
    in_send(small, 1, 0)
    in_send(big, 1, 0)
    in_send(small, 0, 1)
    ring_start(small, 0)
    ring_start(big, 0)
    ring_start(small, 1)
    small.ring_step(0, 1)
    in_send(small, 1, 1)
    in_send(big, 0, 1)
    swap_start(big, 0)
    big.ring_step(0, 1)
    swap_start(small, 0)
    small.ring_step(0, 2)
    small.ring_step(1, 1)
    swap_start(small, 1)
    big.ring_step(0, 2)
    big.s_compute(0)
    ring_start(big, 1)
    small.ring_step(0, 3)
    in_send(big, 1, 1)
    big.s_core(0)
    small.ring_step(0, 4)
    small.s_compute(0)
    small.ring_step(1, 2)
    small.s_core(0)
    big.s_reduce(0)
    swap_start(big, 1)
    small.ring_step(1, 3)
    big.ring_step(1, 1)
    small.s_reduce(0)
    small.ring_step(1, 4)
    small.s_compute(1)
    big.p_compute(0)
    big.ring_step(1, 2)
    small.s_core(1)
    small.p_compute(0)
    big.s_compute(1)
    small.out_compute(0)
    big.p_forward(0)
    big.s_core(1)
    big.out_compute(0)
    small.rs_send(0, 2)
    small.s_reduce(1)
    big.rs_send(0, 2)
    small.rs_send(0, 3)
    big.s_reduce(1)
    small.p_compute(1)
    small.out_compute(1)
    big.p_compute(1)
    small.rs_send(0, 4)
    big.edge_start(0)
    small.rs_send(1, 2)
    big.rs_end(0)
    big.out_part(3, 0)
    big.out_part(3, 1)
    big.p_forward(1)
    big.out_part(3, 2)
    big.out_part(3, 3)
    big.out_compute(1)
    big.edge_start(1)
    small.rs_send(1, 3)
    small.edge_start(0)
    big.edge_end(0)
    big.out_part(0, 0)
    big.out_part(0, 1)
    big.rs_send(1, 2)
    big.out_part(0, 2)
    big.out_part(0, 3)
    small.rs_send(1, 4)
    small.edge_start(1)
    big.edge_end(1)
    big.out_part(1, 0)
    big.out_part(1, 1)
    big.out_part(1, 2)
    big.out_part(1, 3)
    big.rs_end(1)
    big.out_part(2, 0)
    big.out_part(2, 1)
    big.out_part(2, 2)
    big.out_part(2, 3)
    small.rs_end(1)
    small.edge_end(1)
    small.edge_end(0)
    small.rs_end(0)

    stores = []
    for index, ref in ((0, a_out), (3, gv_out), (1, gq_out), (2, gk_out)):
        big.out_wait(index)
        small.out_wait(index)
        for m in range(H // 2):
            tile = slice(128 * m, 128 * m + 128)
            first, second = swap_halves(orep[index, 2 * m], orep[index, 2 * m + 1])
            results[index, 0, :, tile] = first
            results[index, 1, :, tile] = second
        stores.append(pltpu.make_async_copy(results.at[index], ref, local_sems.at[4 + index]))
        stores[-1].start()
    net.finish(small.rterm.at[0])
    for copy in stores:
        copy.wait()


def hand_over(*refs):
    sources, targets, held, sems = refs[:4], refs[4:8], refs[8], refs[9]
    reads = [pltpu.make_async_copy(sources[i], held.at[i], sems.at[i]) for i in range(4)]
    writes = [pltpu.make_async_copy(held.at[i], targets[i], sems.at[4 + i]) for i in range(4)]
    for copy in reads:
        copy.start()
    for read, write in zip(reads, writes):
        read.wait()
        write.start()
    for copy in writes:
        copy.wait()


SENDS, RECEIVES = 12, 66


def shards(query_proj, key_proj, value_proj, grad_output):
    row_count = query_proj.shape[0] * lax.axis_size("row")
    factor = 1.0 / math.sqrt(D // H * row_count)
    anywhere = pl.BlockSpec(memory_space=pl.ANY)
    shape = query_proj.shape
    results = pl.pallas_call(
        functools.partial(kernel, factor),
        out_shape=(jax.ShapeDtypeStruct(shape, BF),) * 4,
        in_specs=[anywhere] * 4,
        out_specs=(anywhere,) * 4,
        scratch_shapes=[
            pltpu.VMEM((4, *shape), BF),
            pltpu.VMEM((4, *shape), BF),
            pltpu.VMEM((4, H, C, 128), BF),
            pltpu.VMEM((4, H, C, 128), BF),
            pltpu.SemaphoreType.DMA((SENDS,)),
            pltpu.SemaphoreType.DMA((RECEIVES,)),
            pltpu.SemaphoreType.DMA((8,)),
            *Unit.scratch(NZ, C, True),
            *Unit.scratch(NX, 2 * C, False),
        ],
        compiler_params=pltpu.CompilerParams(
            collective_id=0, has_side_effects=True, vmem_limit_bytes=60 * 2**20
        ),
        cost_estimate=pl.CostEstimate(flops=1_208_000_000, bytes_accessed=1_600_000, transcendentals=50_000),
        name="exchange_and_compute",
    )(query_proj, key_proj, value_proj, grad_output)
    return pl.pallas_call(
        hand_over,
        out_shape=(jax.ShapeDtypeStruct(shape, BF),) * 4,
        in_specs=[anywhere] * 4,
        out_specs=(anywhere,) * 4,
        scratch_shapes=[pltpu.VMEM((4, *shape), BF), pltpu.SemaphoreType.DMA((8,))],
        name="hand_over",
    )(*results)


def solution(mesh):
    placed = P("row", "col", None)
    return jax.shard_map(
        shards,
        mesh=mesh,
        in_specs=(placed,) * 4,
        out_specs=(placed,) * 4,
        check_vma=False,
    )
```
